256 devices in a mesh: seq: 128 (over x_lo, y, z, core), rep: 2 (over x_hi).
Axes of the slice: x: 4 (x_hi: 2, x_lo: 2; x = x_hi * 2 + x_lo), y: 4, z: 8, core: 2. Of those that a mesh axis runs over, the one named last changes fastest.
Arguments:
- tokens: bfloat16 [2, 32768, 2304], P('rep', 'seq'), may hold values from -24 to 24
- window_ids: int32 [2, 32768], P('rep', 'seq'), may hold values from 0 to 1023, as said below
- cotangent: bfloat16 [2, 32768, 2304], P('rep', 'seq'), may hold values from -24 to 24
- modulation: float32 [6, 2304], replicated, may hold values from -4 to 4
- w_qkv: bfloat16 [2, 2304, 768], replicated
- w_out: bfloat16 [2, 256, 2304], replicated, may hold values from -0.375 to 0.375
Outputs:
- grad_tokens: bfloat16 [2, 32768, 2304], P('rep', 'seq')
- grad_qkv: bfloat16 [2, 2304, 768], P(None, ('seq', 'rep'))
- grad_out: bfloat16 [2, 256, 2304], P(None, None, ('seq', 'rep'))
The draws below stay inside these ranges and needn't reach their ends.
Inputs may be any that keep to these rules, and one draw needn't show every extreme that they name: `window_ids`: each id names exactly 64 tokens, all inside one aligned block of 256 tokens of a group; the ids of the b-th such block (groups in order) are b * 4 to (b + 1) * 4 - 1.
All inputs are finite; a program needn't handle non-finite values.
Results may differ from the reference program's by a relative error of at most 0.027.
Values may be sent and summed in bfloat16 or wider, within the bound.
A program may use at most 128 MiB of HBM per device.

```python
import jax
import jax.numpy as jnp
from jax import lax

D = 2304
HD = 128
HEADS = 2
WIN = 64
FRAMES = 8
TOK_DEV = 256
SEQ_TOK = 32768
PIXELS = 4096
REPLICAS = 2
TOK_ALL = 65536


def draw_window_ids(key, part):
    key = jax.random.fold_in(key, 5)
    blocks = REPLICAS * SEQ_TOK // TOK_DEV
    block_keys = jax.random.split(key, blocks)
    orders = jax.vmap(lambda single: jax.random.permutation(single, TOK_DEV))(block_keys)
    starts = jnp.arange(blocks, dtype=jnp.int32)[:, None] * (TOK_DEV // WIN)
    return (starts + orders.astype(jnp.int32) // WIN).reshape(REPLICAS, SEQ_TOK)


def draw_w_qkv(key, part):
    key = jax.random.fold_in(key, 11)
    key_q, key_k, key_v = jax.random.split(key, 3)
    inner_width = HEADS * HD
    full_shape = (2, D, inner_width)
    spread = D ** (-0.5)
    query_w = spread * jax.random.normal(key_q, full_shape, jnp.float32)
    key_w = spread * jax.random.normal(key_k, full_shape, jnp.float32)
    value_w = spread * jax.random.normal(key_v, full_shape, jnp.float32)
    return jnp.concatenate([query_w, key_w, value_w], axis=2).astype(jnp.bfloat16)


def spiked(entries, key, source, target, blocks, factor):
    def block_of(axis_at):
        return (jnp.arange(entries.shape[axis_at]) // (entries.shape[axis_at] // blocks)).reshape((-1,) + (1,) * (entries.ndim - 1 - axis_at))

    one_side = jax.random.permutation(key, blocks)[block_of(target)]
    second = (block_of(target) + blocks // 2) % blocks
    return jnp.where((block_of(source) == one_side) | (block_of(source) == second), factor * entries, entries)


def level_of(rng, shape, cuts, low, largest):
    def one(position, shards_of):
        draws = jax.random.uniform(jax.random.fold_in(jax.random.fold_in(rng, 6), position), (shards_of,), jnp.float32, low / len(cuts), largest / len(cuts))
        return jnp.repeat(jnp.exp(draws), shape[position] // shards_of).reshape((-1,) + (1,) * (len(shape) - position - 1))

    factor_of = one(*cuts[0])
    for cut in cuts[1:]:
        factor_of = factor_of * one(*cut)
    return factor_of


def noise(own_key, dims, scale, limit, pieces=(), kind=jnp.bfloat16):
    drawn = jax.random.normal(own_key, dims, jnp.float32) * scale
    if len(pieces) > 0:
        drawn = level_of(own_key, dims, pieces, -0.22, 0.18) * drawn
    return jnp.clip(drawn, min=-limit, max=limit).astype(kind)


def noise_with(key, extent, scale, most, shards, heavy, kind=jnp.bfloat16):
    values = scale * jax.random.normal(key, extent, jnp.float32)
    if shards:
        values = values * level_of(key, extent, shards, -0.22, 0.18)
    return jnp.clip(spiked(values, jax.random.fold_in(key, 3), *heavy), -most, most).astype(kind)


def setup_inputs(seed: int = 0) -> dict:
    seeds = jax.random.split(jax.random.key(seed), 7)
    tokens = noise_with(seeds[0], (REPLICAS, SEQ_TOK, D), 1.0, 24.0, ((0, 2), (1, 128)), (1, 2, 128, 5.5))
    window_ids = draw_window_ids(jax.random.fold_in(seeds[6], 71), 0)
    cotangent = noise_with(seeds[2], (REPLICAS, SEQ_TOK, D), 1.0, 24.0, ((0, 2), (1, 128)), (1, 2, 128, 5.5))
    modulation = noise(seeds[3], (6, D), 1.0, 4.0, (), jnp.float32)
    w_qkv = draw_w_qkv(jax.random.fold_in(seeds[6], 71), 0)
    w_out = noise(seeds[5], (2, HEADS * HD, D), (HEADS * HD) ** -0.5, 0.375)
    return dict(tokens=tokens, window_ids=window_ids, cotangent=cotangent, modulation=modulation, w_qkv=w_qkv, w_out=w_out)


epsilon = 1e-06

def keep(values):
    return lax.optimization_barrier(values.astype(jnp.bfloat16))

def normalize(values):
    values = values.astype(jnp.float32)
    centered = values - lax.optimization_barrier(jnp.mean(values, axis=-1, keepdims=True))
    inv_std = lax.rsqrt(lax.optimization_barrier(jnp.mean(centered * centered, axis=-1, keepdims=True)) + epsilon)
    return (centered * inv_std, inv_std)

def norm_back(d_normed, normed, inv_std):
    return inv_std * (d_normed - lax.optimization_barrier(jnp.mean(d_normed, axis=-1, keepdims=True)) - normed * lax.optimization_barrier(jnp.mean(d_normed * normed, axis=-1, keepdims=True)))

def split_heads(packed):
    groups, length, width = packed.shape
    parts = packed.astype(jnp.float32).reshape(groups, length, 3, HEADS, HD)
    return (parts[:, :, 0], parts[:, :, 1], parts[:, :, 2])

def attend(packed, mask):
    query, key_part, value_part = split_heads(packed)
    scores = jnp.einsum('gihd,gjhd->ghij', query, key_part) * HD ** (-0.5)
    if mask is not None:
        scores = jnp.where(mask[:, None], scores, -1e+30)
    top_score = lax.optimization_barrier(jnp.max(scores, axis=-1, keepdims=True))
    expd = jnp.exp(scores - top_score)
    attn_probs = expd / lax.optimization_barrier(jnp.sum(expd, axis=-1, keepdims=True))
    rounded = keep(attn_probs).astype(jnp.float32)
    result = jnp.einsum('ghij,gjhd->gihd', rounded, value_part)
    groups, length = (packed.shape[0], packed.shape[1])
    return (keep(result).reshape(groups, length, HEADS * HD), attn_probs)

def attend_back(packed, attn_probs, d_att):
    query, key_part, value_part = split_heads(packed)
    groups, length = (packed.shape[0], packed.shape[1])
    d_heads = d_att.astype(jnp.float32).reshape(groups, length, HEADS, HD)
    rounded = keep(attn_probs).astype(jnp.float32)
    d_value = jnp.einsum('ghij,gihd->gjhd', rounded, d_heads)
    d_prob = jnp.einsum('gihd,gjhd->ghij', d_heads, value_part)
    d_score = attn_probs * (d_prob - lax.optimization_barrier(jnp.sum(attn_probs * d_prob, axis=-1, keepdims=True)))
    d_score = keep(d_score).astype(jnp.float32)
    d_query = jnp.einsum('ghij,gjhd->gihd', d_score, key_part) * HD ** (-0.5)
    d_key = jnp.einsum('ghij,gihd->gjhd', d_score, query) * HD ** (-0.5)
    stacked = jnp.stack([d_query, d_key, d_value], axis=2)
    return keep(stacked).reshape(groups, length, 3 * HEADS * HD)

def block_forward(block_in, mod_rows, weight_in, weight_out, to_groups, from_groups, mask):
    normed, inv_std = normalize(block_in)
    hidden = keep(normed * (1.0 + mod_rows[1]) + mod_rows[0])
    packed = keep(jnp.dot(hidden, weight_in, preferred_element_type=jnp.float32))
    att_groups, attn_probs = attend(to_groups(packed), mask)
    attended = from_groups(att_groups)
    block_out = keep(block_in.astype(jnp.float32) + mod_rows[2] * jnp.dot(attended, weight_out, preferred_element_type=jnp.float32))
    return (block_out, (normed, inv_std, hidden, packed, attended, attn_probs))

def block_backward(d_block, mod_rows, weight_in, weight_out, saved, to_groups, from_groups):
    normed, inv_std, hidden, packed, attended, attn_probs = saved
    gated = keep(mod_rows[2] * d_block.astype(jnp.float32))
    d_att = keep(jnp.dot(gated, weight_out.T, preferred_element_type=jnp.float32))
    sum_out = jnp.dot(attended.T, gated, preferred_element_type=jnp.float32)
    d_packed = from_groups(attend_back(to_groups(packed), attn_probs, to_groups(d_att)))
    sum_qkv = jnp.dot(hidden.T, d_packed, preferred_element_type=jnp.float32)
    d_hidden = jnp.dot(d_packed, weight_in.T, preferred_element_type=jnp.float32)
    d_in = keep(d_block.astype(jnp.float32) + norm_back(d_hidden * (1.0 + mod_rows[1]), normed, inv_std))
    return (d_in, sum_qkv, sum_out)

def window_groups(values):
    return values.reshape(SEQ_TOK // TOK_DEV, TOK_DEV, values.shape[-1])

def window_rows(values):
    return values.reshape(SEQ_TOK, values.shape[-1])

def frame_groups(values):
    return values.reshape(FRAMES, PIXELS, values.shape[-1]).transpose(1, 0, 2)

def frame_rows(values):
    return values.transpose(1, 0, 2).reshape(SEQ_TOK, values.shape[-1])

def reference(tokens, window_ids, cotangent, modulation, w_qkv, w_out):
    grads_in = jnp.zeros((2, D, 3 * HEADS * HD), jnp.float32)
    grads_out = jnp.zeros((2, HEADS * HD, D), jnp.float32)
    results = []
    for replica in range(REPLICAS):
        id_blocks = window_ids[replica].reshape(SEQ_TOK // TOK_DEV, TOK_DEV)
        mask = id_blocks[:, :, None] == id_blocks[:, None, :]
        mid, saved_s = block_forward(tokens[replica], modulation[0:3], w_qkv[0], w_out[0], window_groups, window_rows, mask)
        unused, saved_t = block_forward(mid, modulation[3:6], w_qkv[1], w_out[1], frame_groups, frame_rows, None)
        d_mid, qkv_t, out_t = block_backward(cotangent[replica], modulation[3:6], w_qkv[1], w_out[1], saved_t, frame_groups, frame_rows)
        d_tokens, qkv_s, out_s = block_backward(d_mid, modulation[0:3], w_qkv[0], w_out[0], saved_s, window_groups, window_rows)
        grads_in = grads_in + jnp.stack([qkv_s, qkv_t])
        grads_out = grads_out + jnp.stack([out_s, out_t])
        results.append(d_tokens)
    factor = TOK_ALL ** (-0.5)
    return (jnp.stack(results), (grads_in * factor).astype(jnp.bfloat16), (grads_out * factor).astype(jnp.bfloat16))
```

```python
import math

import jax
import jax.numpy as jnp
from jax import lax
from jax.sharding import PartitionSpec as P

HD = 128
HEADS = 2
FRAMES = 8
epsilon = 1e-06


def normalize(values):
    values = values.astype(jnp.float32)
    centered = values - jnp.mean(values, axis=-1, keepdims=True)
    inv_std = lax.rsqrt(jnp.mean(centered * centered, axis=-1, keepdims=True) + epsilon)
    return (centered * inv_std, inv_std)


def norm_back(d_normed, normed, inv_std):
    return inv_std * (
        d_normed
        - jnp.mean(d_normed, axis=-1, keepdims=True)
        - normed * jnp.mean(d_normed * normed, axis=-1, keepdims=True)
    )


def contract_rows(left, right):
    return lax.dot_general(
        left, right, (((0,), (0,)), ((), ())), preferred_element_type=jnp.float32
    )


def times_transposed(left, right):
    return lax.dot_general(
        left, right, (((1,), (1,)), ((), ())), preferred_element_type=jnp.float32
    )


def dot(left, right):
    return jnp.dot(left, right, preferred_element_type=jnp.float32)


def head(packed, part, h):
    at = (part * HEADS + h) * HD
    return packed[:, at : at + HD]


def attend(packed, mask):
    probs, outs = [], []
    for h in range(HEADS):
        scores = times_transposed(head(packed, 0, h), head(packed, 1, h)) * HD ** (-0.5)
        scores = jnp.where(mask, scores, -1e30)
        expd = jnp.exp(scores - jnp.max(scores, axis=-1, keepdims=True))
        p = expd / jnp.sum(expd, axis=-1, keepdims=True)
        probs.append(p)
        outs.append(dot(p.astype(jnp.bfloat16), head(packed, 2, h)).astype(jnp.bfloat16))
    return jnp.concatenate(outs, axis=1), probs


def attend_back(packed, probs, d_att):
    dq, dk, dv = [], [], []
    for h in range(HEADS):
        p = probs[h]
        d_out = d_att[:, h * HD : (h + 1) * HD]
        dv.append(contract_rows(p.astype(jnp.bfloat16), d_out))
        dp = times_transposed(d_out, head(packed, 2, h))
        ds = p * (dp - jnp.sum(p * dp, axis=-1, keepdims=True))
        ds = ds.astype(jnp.bfloat16)
        dq.append(dot(ds, head(packed, 1, h)) * HD ** (-0.5))
        dk.append(contract_rows(ds, head(packed, 0, h)) * HD ** (-0.5))
    return jnp.concatenate(dq + dk + dv, axis=1).astype(jnp.bfloat16)


def project_in(block_in, mod_rows, weight_in):
    normed, inv_std = normalize(block_in)
    hidden = (normed * (1.0 + mod_rows[1]) + mod_rows[0]).astype(jnp.bfloat16)
    packed = dot(hidden, weight_in).astype(jnp.bfloat16)
    return (normed, inv_std, hidden, packed)


def gate(d_block, mod_rows):
    return (mod_rows[2] * d_block.astype(jnp.float32)).astype(jnp.bfloat16)


def input_side(d_block, d_packed, mod_rows, weight_in, normed, inv_std):
    d_hidden = times_transposed(d_packed, weight_in)
    return (
        d_block.astype(jnp.float32) + norm_back(d_hidden * (1.0 + mod_rows[1]), normed, inv_std)
    ).astype(jnp.bfloat16)


def local(tokens, window_ids, cotangent, modulation, w_qkv, w_out):
    x = tokens[0]
    ids = window_ids[0]
    d_top = cotangent[0]
    rows = x.shape[0]
    seq = lax.axis_size("seq")
    per_frame = seq // FRAMES
    groups = [[b + per_frame * f for f in range(FRAMES)] for b in range(per_frame)]
    mod_s = modulation[0:3]
    mod_t = modulation[3:6]
    mask_s = ids[:, None] == ids[None, :]
    pixel = lax.rem(jnp.arange(rows, dtype=jnp.int32), rows // FRAMES)
    mask_t = pixel[:, None] == pixel[None, :]

    def exchange(values):
        return lax.all_to_all(
            values, "seq", split_axis=0, concat_axis=0, tiled=True, axis_index_groups=groups
        )

    normed_s, inv_s, hidden_s, packed_s = project_in(x, mod_s, w_qkv[0])
    attended_s, probs_s = attend(packed_s, mask_s)
    middle = (
        x.astype(jnp.float32) + mod_s[2] * dot(attended_s, w_out[0])
    ).astype(jnp.bfloat16)
    normed_t, inv_t, hidden_t, packed_t = project_in(middle, mod_t, w_qkv[1])
    gated_t = gate(d_top, mod_t)
    d_att_t = times_transposed(gated_t, w_out[1]).astype(jnp.bfloat16)
    pix = exchange(jnp.concatenate([packed_t, d_att_t], axis=1))
    wide = 3 * HEADS * HD
    attended_p, probs_p = attend(pix[:, :wide], mask_t)
    d_packed_p = attend_back(pix[:, :wide], probs_p, pix[:, wide:])
    back = exchange(jnp.concatenate([d_packed_p, attended_p], axis=1))
    d_packed_t = back[:, :wide]
    attended_t = back[:, wide:]
    d_middle = input_side(d_top, d_packed_t, mod_t, w_qkv[1], normed_t, inv_t)
    gated_s = gate(d_middle, mod_s)
    d_att_s = times_transposed(gated_s, w_out[0]).astype(jnp.bfloat16)
    d_packed_s = attend_back(packed_s, probs_s, d_att_s)
    d_tokens = input_side(d_middle, d_packed_s, mod_s, w_qkv[0], normed_s, inv_s)

    sums = jnp.concatenate(
        [
            contract_rows(hidden_s, d_packed_s),
            contract_rows(hidden_t, d_packed_t),
            contract_rows(gated_s, attended_s),
            contract_rows(gated_t, attended_t),
        ],
        axis=1,
    ).astype(jnp.bfloat16)
    devices = seq * lax.axis_size("rep")
    features, columns = sums.shape
    own = features // devices
    summed = lax.psum_scatter(
        sums.reshape(devices, own * columns), ("seq", "rep"), scatter_dimension=0, tiled=True
    ).reshape(own, columns).astype(jnp.float32)
    factor = 1.0 / math.sqrt(rows * devices)
    summed = (summed * factor).astype(jnp.bfloat16)
    grad_qkv = jnp.stack([summed[:, :wide], summed[:, wide : 2 * wide]])
    outs = summed[:, 2 * wide :].reshape(own, 2, HEADS * HD)
    return (d_tokens[None], grad_qkv, outs.transpose(1, 2, 0))


def solution(mesh):
    in_specs = (P("rep", "seq", None), P("rep", "seq"), P("rep", "seq", None), P(), P(), P())
    out_specs = (
        P("rep", "seq", None),
        P(None, ("seq", "rep"), None),
        P(None, None, ("seq", "rep")),
    )
    return jax.shard_map(local, mesh=mesh, in_specs=in_specs, out_specs=out_specs, check_vma=False)
```

```python
import math

import jax
import jax.numpy as jnp
from jax import lax
from jax.experimental import pallas as pl
from jax.experimental.pallas import tpu as pltpu
from jax.sharding import PartitionSpec as P

HD = 128
HEADS = 2
FRAMES = 8
epsilon = 1e-06
MESH = pl.DeviceIdType.MESH


def normalize(values):
    values = values.astype(jnp.float32)
    centered = values - jnp.mean(values, axis=-1, keepdims=True)
    inv_std = lax.rsqrt(jnp.mean(centered * centered, axis=-1, keepdims=True) + epsilon)
    return (centered * inv_std, inv_std)


def norm_back(d_normed, normed, inv_std):
    return inv_std * (
        d_normed
        - jnp.mean(d_normed, axis=-1, keepdims=True)
        - normed * jnp.mean(d_normed * normed, axis=-1, keepdims=True)
    )


def contract_rows(left, right):
    return lax.dot_general(
        left, right, (((0,), (0,)), ((), ())), preferred_element_type=jnp.float32
    )


def times_transposed(left, right):
    return lax.dot_general(
        left, right, (((1,), (1,)), ((), ())), preferred_element_type=jnp.float32
    )


def dot(left, right):
    return jnp.dot(left, right, preferred_element_type=jnp.float32)


def head(packed, part, h):
    at = (part * HEADS + h) * HD
    return packed[:, at : at + HD]


def attend(packed, mask):
    probs, outs = [], []
    for h in range(HEADS):
        scores = times_transposed(head(packed, 0, h), head(packed, 1, h)) * HD ** (-0.5)
        scores = jnp.where(mask, scores, -1e30)
        expd = jnp.exp(scores - jnp.max(scores, axis=-1, keepdims=True))
        p = expd / jnp.sum(expd, axis=-1, keepdims=True)
        probs.append(p)
        outs.append(dot(p.astype(jnp.bfloat16), head(packed, 2, h)).astype(jnp.bfloat16))
    return jnp.concatenate(outs, axis=1), probs


def attend_back(packed, probs, d_att):
    dq, dk, dv = [], [], []
    for h in range(HEADS):
        p = probs[h]
        d_out = d_att[:, h * HD : (h + 1) * HD]
        dv.append(contract_rows(p.astype(jnp.bfloat16), d_out))
        dp = times_transposed(d_out, head(packed, 2, h))
        ds = p * (dp - jnp.sum(p * dp, axis=-1, keepdims=True))
        ds = ds.astype(jnp.bfloat16)
        dq.append(dot(ds, head(packed, 1, h)) * HD ** (-0.5))
        dk.append(contract_rows(ds, head(packed, 0, h)) * HD ** (-0.5))
    return jnp.concatenate(dq + dk + dv, axis=1).astype(jnp.bfloat16)


def project_in(block_in, mod_rows, weight_in):
    normed, inv_std = normalize(block_in)
    hidden = (normed * (1.0 + mod_rows[1]) + mod_rows[0]).astype(jnp.bfloat16)
    packed = dot(hidden, weight_in).astype(jnp.bfloat16)
    return (normed, inv_std, hidden, packed)


def gate(d_block, mod_rows):
    return (mod_rows[2] * d_block.astype(jnp.float32)).astype(jnp.bfloat16)


def input_side(d_block, d_packed, mod_rows, weight_in, normed, inv_std):
    d_hidden = times_transposed(d_packed, weight_in)
    return (
        d_block.astype(jnp.float32) + norm_back(d_hidden * (1.0 + mod_rows[1]), normed, inv_std)
    ).astype(jnp.bfloat16)


X_ROWS, Z_ROWS = 64, 16
BLOCK_ROWS = 288
OWN = 9


def reduce_kernel(t_ref, out_ref, xa, xc, xm, xb, xu, ya, yc, ym, yb, yu,
                  x2, x2m, x2v, y2, y2m, y2v, tz, zr, zu, zx, zxm, zxv, zy, zym,
                  last_out, last_in, spread, gather, final,
                  send_sem, recv_sem):
    seq = lax.axis_index("seq")
    x_hi = lax.axis_index("rep")
    core = lax.rem(seq, 2)
    z = lax.rem(lax.div(seq, 2), 8)
    y = lax.rem(lax.div(seq, 16), 4)
    x_lo = lax.div(seq, 64)
    x = 2 * x_hi + x_lo
    bf16, f32 = jnp.bfloat16, jnp.float32

    def device(x_at, y_at, z_at, core_at):
        return {"seq": ((lax.rem(x_at, 2) * 4 + y_at) * 8 + z_at) * 2 + core_at, "rep": lax.div(x_at, 2)}

    def turn(at, step, size):
        return lax.rem(at + step + size, size)

    x_right, x_left = device(turn(x, 1, 4), y, z, core), device(turn(x, 3, 4), y, z, core)
    y_right, y_left = device(x, turn(y, 1, 4), z, core), device(x, turn(y, 3, 4), z, core)
    z_peers = [device(x, y, turn(z, k, 8), core) for k in range(1, 8)]
    x_far = turn(x, 2, 4)
    mates = [device(x, y, z, 1 - core), device(x_far, y, z, core), device(x_far, y, z, 1 - core)]

    barrier = pltpu.get_barrier_semaphore()
    peers = [x_right, x_left, y_right, y_left] + z_peers + mates
    for peer in peers:
        pl.semaphore_signal(barrier, inc=1, device_id=peer, device_id_type=MESH)
    pl.semaphore_wait(barrier, len(peers))

    used = []

    def send(src, dst, peer):
        at = len(used)
        copy = pltpu.make_async_remote_copy(
            src_ref=src, dst_ref=dst, send_sem=send_sem.at[at], recv_sem=recv_sem.at[at],
            device_id=peer, device_id_type=MESH,
        )
        copy.start()
        used.append(copy)
        return copy

    def rows(x_at, y_at, offset, size):
        start = (lax.rem(x_at, 2) * 4 + y_at) * BLOCK_ROWS + offset + size * lax.div(x_at, 2)
        return pl.ds(pl.multiple_of(start, 16), size)

    def x_src(a, b):
        return t_ref.at[rows(a, b, 0, X_ROWS)]

    def y_src(a, b):
        return t_ref.at[rows(b, a, 2 * X_ROWS, X_ROWS)]

    def far_sends(me, src, box, right, left):
        far = turn(me, 2, 4)
        a = [send(src(far, b), box.at[0, b], right) for b in (0, 1)]
        c = [send(src(far, b), box.at[0, b], left) for b in (2, 3)]
        return a, c

    def near_sends(me, src, box, right, left):
        a = [send(src(turn(me, 1, 4), b), box.at[b], right) for b in (2, 3)]
        c = [send(src(turn(me, 3, 4), b), box.at[b], left) for b in (0, 1)]
        return a + c

    def relay(me, src, box, mid, into, far, right, left):
        outs = []
        for n in range(2):
            far[0][n].wait_recv()
            mid[n] = (box[0, n].astype(f32) + src(turn(me, 1, 4), n)[...].astype(f32)).astype(bf16)
            outs.append(send(mid.at[n], into.at[n], right))
            far[1][n].wait_recv()
            mid[n + 2] = (box[0, n + 2].astype(f32) + src(turn(me, 3, 4), n + 2)[...].astype(f32)).astype(bf16)
            outs.append(send(mid.at[n + 2], into.at[n + 2], left))
        return outs

    def finish(me, src, near, into, copies, total):
        for copy in copies:
            copy.wait_recv()
        for b in range(4):
            total[b] = (src(me, b)[...].astype(f32) + near[b].astype(f32) + into[b].astype(f32)).astype(bf16)

    x_far_sends = far_sends(x, x_src, xa, x_right, x_left)
    y_far_sends = far_sends(y, y_src, ya, y_right, y_left)
    for u in range(8):
        for a in range(4):
            for b in range(4):
                tz[u, a, b] = t_ref[pl.ds((a % 2 * 4 + b) * BLOCK_ROWS + 4 * X_ROWS + Z_ROWS * (a // 2), Z_ROWS), pl.ds(u * HD, HD)]
    z_sends = [send(tz.at[turn(z, k, 8)], zr.at[k - 1], z_peers[k - 1]) for k in (4, 3, 5, 2, 6, 1, 7)]
    x_near = near_sends(x, x_src, xb, x_right, x_left)
    y_near = near_sends(y, y_src, yb, y_right, y_left)
    x_relays = relay(x, x_src, xa, xm, xc, x_far_sends, x_right, x_left)
    y_relays = relay(y, y_src, ya, ym, yc, y_far_sends, y_right, y_left)

    def second_start(me, held, box, right, left):
        half = X_ROWS // 2
        far = turn(me, 2, 4)
        lo, hi = pl.ds(0, half), pl.ds(half, half)
        return [
            send(held.at[far, lo], box.at[0, lo], right),
            send(held.at[far, hi], box.at[0, hi], left),
            send(held.at[turn(me, 1, 4), hi], box.at[1, hi], right),
            send(held.at[turn(me, 3, 4), lo], box.at[1, lo], left),
        ]

    def second_relay(me, held, box, mid, copies, right, left):
        half = X_ROWS // 2
        lo, hi = pl.ds(0, half), pl.ds(half, half)
        copies[0].wait_recv()
        mid[lo, :] = (box[0, lo, :].astype(f32) + held[turn(me, 1, 4), lo, :].astype(f32)).astype(bf16)
        one = send(mid.at[lo], box.at[2, lo], right)
        copies[1].wait_recv()
        mid[hi, :] = (box[0, hi, :].astype(f32) + held[turn(me, 3, 4), hi, :].astype(f32)).astype(bf16)
        two = send(mid.at[hi], box.at[2, hi], left)
        return [one, two]

    def second_finish(me, held, box, copies, offset):
        for copy in copies:
            copy.wait_recv()
        total = (held[me].astype(f32) + box[1].astype(f32) + box[2].astype(f32)).astype(bf16)
        for u in range(8):
            last_out[u, pl.ds(offset, X_ROWS), :] = total[:, u * HD : (u + 1) * HD]

    finish(x, x_src, xb, xc, x_near + x_relays, xu)
    x_second = second_start(y, xu, x2, y_right, y_left)
    finish(y, y_src, yb, yc, y_near + y_relays, yu)
    y_second = second_start(x, yu, y2, x_right, x_left)
    for copy in z_sends:
        copy.wait_recv()
    zsum = tz[z].astype(f32)
    for k in range(7):
        zsum = zsum + zr[k].astype(f32)
    zu[...] = zsum.astype(bf16)
    far, right_at, left_at = turn(x, 2, 4), turn(x, 1, 4), turn(x, 3, 4)
    lo, hi = pl.ds(0, 2), pl.ds(2, 2)
    z_first = [
        send(zu.at[far, lo], zx.at[0, lo], x_right),
        send(zu.at[far, hi], zx.at[0, hi], x_left),
        send(zu.at[right_at, hi], zx.at[1, hi], x_right),
        send(zu.at[left_at, lo], zx.at[1, lo], x_left),
    ]
    x_second_more = second_relay(y, xu, x2, x2m, x_second, y_right, y_left)
    y_second_more = second_relay(x, yu, y2, y2m, y_second, x_right, x_left)
    z_first[0].wait_recv()
    zxm[lo] = (zx[0, lo].astype(f32) + zu[right_at, lo].astype(f32)).astype(bf16)
    z_first.append(send(zxm.at[lo], zx.at[2, lo], x_right))
    z_first[1].wait_recv()
    zxm[hi] = (zx[0, hi].astype(f32) + zu[left_at, hi].astype(f32)).astype(bf16)
    z_first.append(send(zxm.at[hi], zx.at[2, hi], x_left))
    for copy in z_first[2:]:
        copy.wait_recv()
    zxv[...] = (zu[x].astype(f32) + zx[1].astype(f32) + zx[2].astype(f32)).astype(bf16)
    z_second = [
        send(zxv.at[turn(y, 2, 4)], zy.at[0], y_right),
        send(zxv.at[turn(y, 3, 4)], zy.at[1], y_left),
    ]
    second_finish(y, xu, x2, x_second[2:] + x_second_more, 0)
    second_finish(x, yu, y2, y_second[2:] + y_second_more, X_ROWS)
    last_sends = [
        send(last_out.at[turn(z, k, 8)], last_in.at[k - 1], z_peers[k - 1]) for k in (4, 3, 5, 2, 6, 1, 7)
    ]
    z_second[0].wait_recv()
    zym[...] = (zy[0].astype(f32) + zxv[turn(y, 1, 4)].astype(f32)).astype(bf16)
    z_second.append(send(zym, zy.at[2], y_right))
    for copy in z_second[1:]:
        copy.wait_recv()
    z_total = zxv[y].astype(f32) + zy[1].astype(f32) + zy[2].astype(f32)
    for copy in last_sends:
        copy.wait_recv()
    total = last_out[z].astype(f32)
    for k in range(7):
        total = total + last_in[k].astype(f32)
    total = jnp.concatenate([total, z_total], axis=0).astype(bf16)

    slots, held_rows = 8 * 4 * 16, 2 * X_ROWS + Z_ROWS
    slot = lax.broadcasted_iota(jnp.int32, (slots, held_rows), 0)
    at = lax.broadcasted_iota(jnp.int32, (slots, held_rows), 1)
    have = jnp.where(
        at < X_ROWS, at + X_ROWS * x_hi,
        jnp.where(at < 2 * X_ROWS, at + X_ROWS + X_ROWS * x_hi, at + 2 * X_ROWS + Z_ROWS * x_hi),
    )
    within = lax.bitwise_and(slot, 15)
    want = lax.shift_right_logical(slot, 4) * OWN + within
    pick = jnp.where((have == want) & (within < OWN), 1.0, 0.0).astype(bf16)
    spread[...] = jnp.dot(pick, total, preferred_element_type=f32).astype(bf16).reshape(8, 64, HD)
    gather_sends = [
        send(spread.at[turn(z, k, 8)], gather.at[z], z_peers[k - 1]) for k in (4, 3, 5, 2, 6, 1, 7)
    ]
    gather[z] = spread[z]
    for copy in gather_sends:
        copy.wait_recv()
    mine = core * 2 + x_hi
    final_sends = []
    for n, (mate_core, mate_hi) in enumerate([(1 - core, x_hi), (core, 1 - x_hi), (1 - core, 1 - x_hi)]):
        place = pl.ds(pl.multiple_of((mate_core * 2 + mate_hi) * 16, 16), 16)
        final_sends.append(send(gather.at[:, place], final.at[n], mates[n]))
    for copy in final_sends:
        copy.wait_recv()
    place = pl.ds(pl.multiple_of(mine * 16, 16), 16)
    own = gather[:, place, :].astype(f32) + final[1].astype(f32)
    other = final[0].astype(f32) + final[2].astype(f32)
    out_ref[core] = own
    out_ref[1 - core] = other
    for copy in used:
        copy.wait_send()


def reduce_scatter(t):
    bf16 = jnp.bfloat16
    wide = 8 * HD
    ring = [
        pltpu.VMEM((1, 4, X_ROWS, wide), bf16),
        pltpu.VMEM((4, X_ROWS, wide), bf16),
        pltpu.VMEM((4, X_ROWS, wide), bf16),
        pltpu.VMEM((4, X_ROWS, wide), bf16),
        pltpu.VMEM((4, X_ROWS, wide), bf16),
    ]
    second = [
        pltpu.VMEM((3, X_ROWS, wide), bf16),
        pltpu.VMEM((X_ROWS, wide), bf16),
        pltpu.VMEM((X_ROWS, wide), bf16),
    ]
    scratch = ring + ring + second + second + [
        pltpu.VMEM((8, 4, 4, Z_ROWS, HD), bf16),
        pltpu.VMEM((7, 4, 4, Z_ROWS, HD), bf16),
        pltpu.VMEM((4, 4, Z_ROWS, HD), bf16),
        pltpu.VMEM((3, 4, Z_ROWS, HD), bf16),
        pltpu.VMEM((4, Z_ROWS, HD), bf16),
        pltpu.VMEM((4, Z_ROWS, HD), bf16),
        pltpu.VMEM((3, Z_ROWS, HD), bf16),
        pltpu.VMEM((Z_ROWS, HD), bf16),
        pltpu.VMEM((8, 2 * X_ROWS, HD), bf16),
        pltpu.VMEM((7, 2 * X_ROWS, HD), bf16),
        pltpu.VMEM((8, 64, HD), bf16),
        pltpu.VMEM((8, 64, HD), bf16),
        pltpu.VMEM((3, 8, 16, HD), bf16),
        pltpu.SemaphoreType.DMA((80,)),
        pltpu.SemaphoreType.DMA((80,)),
    ]
    return pl.pallas_call(
        reduce_kernel,
        out_shape=jax.ShapeDtypeStruct((2, 8, 16, HD), jnp.float32),
        in_specs=[pl.BlockSpec(memory_space=pltpu.VMEM)],
        out_specs=pl.BlockSpec(memory_space=pltpu.VMEM),
        scratch_shapes=scratch,
        compiler_params=pltpu.CompilerParams(
            collective_id=0, has_side_effects=True, vmem_limit_bytes=50 * 2**20
        ),
    )(t)


def local(tokens, window_ids, cotangent, modulation, w_qkv, w_out):
    x = tokens[0]
    ids = window_ids[0]
    d_top = cotangent[0]
    rows = x.shape[0]
    seq = lax.axis_size("seq")
    per_frame = seq // FRAMES
    groups = [[b + per_frame * f for f in range(FRAMES)] for b in range(per_frame)]
    mod_s = modulation[0:3]
    mod_t = modulation[3:6]
    mask_s = ids[:, None] == ids[None, :]
    pixel = lax.rem(jnp.arange(rows, dtype=jnp.int32), rows // FRAMES)
    mask_t = pixel[:, None] == pixel[None, :]

    def exchange(values):
        return lax.all_to_all(
            values, "seq", split_axis=0, concat_axis=0, tiled=True, axis_index_groups=groups
        )

    normed_s, inv_s, hidden_s, packed_s = project_in(x, mod_s, w_qkv[0])
    attended_s, probs_s = attend(packed_s, mask_s)
    middle = (
        x.astype(jnp.float32) + mod_s[2] * dot(attended_s, w_out[0])
    ).astype(jnp.bfloat16)
    normed_t, inv_t, hidden_t, packed_t = project_in(middle, mod_t, w_qkv[1])
    gated_t = gate(d_top, mod_t)
    d_att_t = times_transposed(gated_t, w_out[1]).astype(jnp.bfloat16)
    pix = exchange(jnp.concatenate([packed_t, d_att_t], axis=1))
    wide = 3 * HEADS * HD
    attended_p, probs_p = attend(pix[:, :wide], mask_t)
    d_packed_p = attend_back(pix[:, :wide], probs_p, pix[:, wide:])
    back = exchange(jnp.concatenate([d_packed_p, attended_p], axis=1))
    d_packed_t = back[:, :wide]
    attended_t = back[:, wide:]
    d_middle = input_side(d_top, d_packed_t, mod_t, w_qkv[1], normed_t, inv_t)
    gated_s = gate(d_middle, mod_s)
    d_att_s = times_transposed(gated_s, w_out[0]).astype(jnp.bfloat16)
    d_packed_s = attend_back(packed_s, probs_s, d_att_s)
    d_tokens = input_side(d_middle, d_packed_s, mod_s, w_qkv[0], normed_s, inv_s)

    core = lax.rem(lax.axis_index("seq"), 2)
    pairs = [(n, n + 1 - 2 * (n % 2)) for n in range(seq)]

    def sibling(values):
        return lax.ppermute(values, "seq", pairs)

    def of_head(values, parts, h):
        heads = values.reshape(rows, parts, HEADS, HD)
        return jnp.where(h == 0, heads[:, :, 0], heads[:, :, 1]).reshape(rows, parts * HD)

    def pooled(left, right, parts):
        left2 = jnp.concatenate([left, sibling(left)], axis=0)
        right2 = jnp.concatenate(
            [of_head(right, parts, core), sibling(of_head(right, parts, 1 - core))], axis=0
        )
        return contract_rows(left2, right2)

    sums = jnp.concatenate(
        [
            pooled(hidden_s, d_packed_s, 3),
            pooled(gated_s, attended_s, 1),
            pooled(hidden_t, d_packed_t, 3),
            pooled(gated_t, attended_t, 1),
        ],
        axis=1,
    ).astype(jnp.bfloat16)
    devices = seq * lax.axis_size("rep")
    factor = 1.0 / math.sqrt(rows * devices)
    summed = (reduce_scatter(sums)[:, :, :OWN] * factor).astype(jnp.bfloat16)
    summed = summed.reshape(HEADS, 2, 4, OWN, HD)
    grad_qkv = summed[:, :, :3].transpose(1, 3, 2, 0, 4).reshape(2, OWN, wide)
    grad_out = summed[:, :, 3].transpose(1, 0, 3, 2).reshape(2, HEADS * HD, OWN)
    return (d_tokens[None], grad_qkv, grad_out)


def solution(mesh):
    in_specs = (P("rep", "seq", None), P("rep", "seq"), P("rep", "seq", None), P(), P(), P())
    out_specs = (
        P("rep", "seq", None),
        P(None, ("seq", "rep"), None),
        P(None, None, ("seq", "rep")),
    )
    return jax.shard_map(local, mesh=mesh, in_specs=in_specs, out_specs=out_specs, check_vma=False)
```

```python
import math

import jax
import jax.numpy as jnp
from jax import lax
from jax.experimental import pallas as pl
from jax.experimental.pallas import tpu as pltpu
from jax.sharding import PartitionSpec as P

MESH = pl.DeviceIdType.MESH
BF16, F32 = jnp.bfloat16, jnp.float32
HD = 128
HEADS = 2
FRAMES = 8
UNITS = 4
WIDE = UNITS * HD
BLOCK_ROWS = 288
X_ROWS, Z_ROWS = 64, 16
OWN = 9
SLOT = 16
epsilon = 1e-06
factor_of_scores = HD ** (-0.5)


def nn(left, right):
    return lax.dot_general(left, right, (((1,), (0,)), ((), ())), preferred_element_type=F32)


def nt(left, right):
    return lax.dot_general(left, right, (((1,), (1,)), ((), ())), preferred_element_type=F32)


def softmax(query, key, mask):
    scores = jnp.where(mask, nt(query, key) * factor_of_scores, -1e30)
    expd = jnp.exp(scores - jnp.max(scores, axis=-1, keepdims=True))
    return expd / jnp.sum(expd, axis=-1, keepdims=True)


def attend_back(query, key, value, probs, d_out):
    d_value = nn(probs.astype(BF16).T, d_out)
    d_prob = nt(d_out, value)
    d_score = (probs * (d_prob - jnp.sum(probs * d_prob, axis=-1, keepdims=True))).astype(BF16)
    d_query = nn(d_score, key) * factor_of_scores
    d_key = nn(d_score.T, query) * factor_of_scores
    return d_query.astype(BF16), d_key.astype(BF16), d_value.astype(BF16)


def normalize(values):
    centered = values - jnp.mean(values, axis=-1, keepdims=True)
    inv_std = lax.rsqrt(jnp.mean(centered * centered, axis=-1, keepdims=True) + epsilon)
    return centered * inv_std, inv_std


def norm_back(d_normed, normed, inv_std):
    return inv_std * (
        d_normed
        - jnp.mean(d_normed, axis=-1, keepdims=True)
        - normed * jnp.mean(d_normed * normed, axis=-1, keepdims=True)
    )


def whole_kernel(tokens_hbm, ids_ref, cot_hbm, mod_ref, qkv_hbm, out_hbm,
                 grad_ref, sums_ref,
                 x_ref, cot_ref, w0, w1, wo0, wo1,
                 hid0, hid1, mid, g1, g0, acc, pk0, probs, att0,
                 ht0, ht1, gt0, gt1, sib_ht0, sib_ht1, sib_gt0, sib_gt1,
                 out_s, in_s, out_p, back, dp, b0, sib_b1, sib_b0,
                 *rest):
    per_block = 22
    boxes = [rest[:per_block], rest[per_block : 2 * per_block]]
    spread, gather, merged, final, load_sem, send_sem, recv_sem = rest[2 * per_block :]

    seq = lax.axis_index("seq")
    x_hi = lax.axis_index("rep")
    core = lax.rem(seq, 2)
    z = lax.rem(lax.div(seq, 2), 8)
    y = lax.rem(lax.div(seq, 16), 4)
    x_lo = lax.div(seq, 64)
    x = 2 * x_hi + x_lo
    frame = x_lo * 4 + y

    loads = []
    for n, (src, dst) in enumerate([
        (tokens_hbm.at[0], x_ref), (qkv_hbm.at[0], w0), (out_hbm.at[0], wo0),
        (cot_hbm.at[0], cot_ref), (out_hbm.at[1], wo1), (qkv_hbm.at[1], w1),
    ]):
        loads.append(pltpu.make_async_copy(src, dst, load_sem.at[n]))
        loads[n].start()

    def device(x_at, y_at, z_at, core_at):
        return {"seq": ((lax.rem(x_at, 2) * 4 + y_at) * 8 + z_at) * 2 + core_at, "rep": lax.div(x_at, 2)}

    def turn(at, step, size):
        return lax.rem(at + step, size)

    x_right, x_left = device(turn(x, 1, 4), y, z, core), device(turn(x, 3, 4), y, z, core)
    x_far_at = turn(x, 2, 4)
    z_order = (4, 3, 5, 2, 6, 1, 7)
    z_peers = {k: device(x, y, turn(z, k, 8), core) for k in z_order}
    mates = [device(x, y, z, 1 - core), device(x_far_at, y, z, core), device(x_far_at, y, z, 1 - core)]
    sibling, x_far = mates[0], mates[1]
    other = 2 * x_hi + 1 - x_lo
    clip = []
    for cross, step in ((1, 2), (1, 1), (1, 3), (1, 0), (0, 2), (0, 1), (0, 3)):
        y_at = turn(y, step, 4)
        frame_at = (1 - x_lo if cross else x_lo) * 4 + y_at
        clip.append((frame_at, device(other if cross else x, y_at, z, core)))
    y_far, y_right, y_left = clip[4][1], clip[5][1], clip[6][1]

    barrier = pltpu.get_barrier_semaphore()
    peers = [x_right, x_left] + mates + list(z_peers.values()) + [peer for _, peer in clip]
    for peer in peers:
        pl.semaphore_signal(barrier, inc=1, device_id=peer, device_id_type=MESH)

    used = []

    def send(src, dst, peer):
        at = len(used)
        copy = pltpu.make_async_remote_copy(
            src_ref=src, dst_ref=dst, send_sem=send_sem.at[at], recv_sem=recv_sem.at[at],
            device_id=peer, device_id_type=MESH,
        )
        copy.start()
        used.append(copy)
        return copy

    def arrived(copies):
        for copy in copies:
            copy.wait_recv()

    rows_of = x_ref.shape[0]
    features = x_ref.shape[1]
    shift0, scale0, gate0, shift1, scale1, gate1 = range(6)

    def mod(n):
        return mod_ref[n : n + 1, :]

    def by_rows(body):
        def step(i, carry):
            body(pl.ds(pl.multiple_of(i * 16, 16), 16))
            return carry

        lax.fori_loop(0, rows_of // 16, step, 0)

    def by_columns(body, size=256):
        def step(i, carry):
            body(pl.ds(pl.multiple_of(i * size, size), size))
            return carry

        lax.fori_loop(0, features // size, step, 0)

    loads[0].wait()

    def spatial_in(at):
        normed, _ = normalize(x_ref[at, :].astype(F32))
        hid0[at, :] = (normed * (1.0 + mod(scale0)) + mod(shift0)).astype(BF16)

    by_rows(spatial_in)
    loads[1].wait()

    def project0(i, carry):
        at = pl.ds(pl.multiple_of(i * 256, 256), 256)
        pk0[:, at] = nn(hid0[...], w0[:, at]).astype(BF16)
        return carry

    lax.fori_loop(0, 3, project0, 0)

    ids = jnp.broadcast_to(ids_ref[...], (rows_of, rows_of))
    mask = ids == ids.T

    def part(n, h):
        return pk0[:, (2 * n + h) * HD : (2 * n + h + 1) * HD]

    for h in range(HEADS):
        p = softmax(part(0, h), part(1, h), mask)
        probs[h] = p
        att = nn(p.astype(BF16), part(2, h)).astype(BF16)
        att0[:, h * HD : (h + 1) * HD] = att
        b0[h, :, 3 * HD :] = att
    loads[2].wait()

    def middle(at):
        mid[:, at] = (
            x_ref[:, at].astype(F32) + mod_ref[gate0 : gate0 + 1, at] * nn(att0[...], wo0[:, at])
        ).astype(BF16)

    by_columns(middle)

    def temporal_in(at):
        normed, _ = normalize(mid[at, :].astype(F32))
        hid1[at, :] = (normed * (1.0 + mod(scale1)) + mod(shift1)).astype(BF16)

    by_rows(temporal_in)
    loads[3].wait()

    def gate_top(at):
        g1[at, :] = (mod(gate1) * cot_ref[at, :].astype(F32)).astype(BF16)

    by_rows(gate_top)
    loads[4].wait()
    d_att1 = nt(g1[...], wo1[...]).astype(BF16)
    for h in range(HEADS):
        out_s[h, :, 3 * HD :] = d_att1[:, h * HD : (h + 1) * HD]
    loads[5].wait()

    def project1(i, carry):
        packed = nn(hid1[...], w1[:, pl.ds(pl.multiple_of(i * 256, 256), 256)]).astype(BF16)
        at = pl.ds(pl.multiple_of(i * HD, HD), HD)
        for h in range(HEADS):
            out_s[h, :, at] = packed[:, h * HD : (h + 1) * HD]
        return carry

    lax.fori_loop(0, 3, project1, 0)

    pixels = rows_of // FRAMES

    def pixel_rows(n):
        return pl.ds(pl.multiple_of(n * pixels, pixels), pixels)

    pl.semaphore_wait(barrier, len(peers))
    gone = [
        [send(out_s.at[h, pixel_rows(at)], in_s.at[h, frame], peer) for at, peer in clip]
        for h in range(HEADS)
    ]

    def flip(src, dst):
        def body(at):
            dst[at, :] = src[:, at].T

        by_columns(body)

    flip(hid1, ht1)
    shared1 = [send(ht1, sib_ht1, sibling)]
    flip(g1, gt1)
    shared1.append(send(gt1, sib_gt1, sibling))

    pixel_row = lax.bitwise_and(lax.broadcasted_iota(jnp.int32, (rows_of, rows_of), 0), pixels - 1)
    pixel_col = lax.bitwise_and(lax.broadcasted_iota(jnp.int32, (rows_of, rows_of), 1), pixels - 1)
    same_pixel = pixel_row == pixel_col
    came = []
    for h in range(HEADS):
        in_s[h, frame] = out_s[h, pixel_rows(frame), :]
        arrived(gone[h])
        block = in_s[h].reshape(rows_of, WIDE)
        query, key, value, d_out = [block[:, n * HD : (n + 1) * HD] for n in range(UNITS)]
        p = softmax(query, key, same_pixel)
        out_p[h, :, 3 * HD :] = nn(p.astype(BF16), value).astype(BF16)
        for n, part_of in enumerate(attend_back(query, key, value, p, d_out)):
            out_p[h, :, n * HD : (n + 1) * HD] = part_of
        came.append([
            send(out_p.at[h, pixel_rows(at)], back.at[h, pixel_rows(frame)], peer) for at, peer in clip
        ])
    flip(hid0, ht0)
    shared0 = [send(ht0, sib_ht0, sibling)]
    for h in range(HEADS):
        back[h, pixel_rows(frame), :] = out_p[h, pixel_rows(frame), :]
        arrived(came[h])
    shared1.append(send(back.at[1 - core], sib_b1, sibling))

    def reduction(box, t):
        (_, xa, xc, xm, xb, xu, ya, yc, ym, yb, yu, x2, x2m, y2, y2m, tz, zr, zu, zx, zy, last_out, last_in) = box

        def rows(x_at, y_at, offset):
            start = (lax.rem(x_at, 2) * 4 + y_at) * BLOCK_ROWS + offset + X_ROWS * lax.div(x_at, 2)
            return pl.ds(pl.multiple_of(start, 16), X_ROWS)

        def x_src(a, b):
            return t.at[rows(a, b, 0)]

        def y_src(a, b):
            return t.at[rows(b, a, 2 * X_ROWS)]

        def total2(one, two):
            return (one.astype(F32) + two.astype(F32)).astype(BF16)

        def far_sends(me, src, into, right, left):
            far = turn(me, 2, 4)
            return (
                [send(src(far, b), into.at[b], right) for b in (0, 1)]
                + [send(src(far, b), into.at[b], left) for b in (2, 3)]
            )

        def near_sends(me, src, into, right, left):
            return (
                [send(src(turn(me, 1, 4), b), into.at[b], right) for b in (2, 3)]
                + [send(src(turn(me, 3, 4), b), into.at[b], left) for b in (0, 1)]
            )

        def relay(me, src, box_in, kept, into, far, right, left):
            outs = []
            for n in (0, 2, 1, 3):
                far[n].wait_recv()
                kept[n] = total2(box_in[n], src(turn(me, 1 if n < 2 else 3, 4), n)[...])
                outs.append(send(kept.at[n], into.at[n], right if n < 2 else left))
            return outs

        def finish(me, src, near, into, copies, result):
            arrived(copies)
            for b in range(4):
                result[b] = (
                    src(me, b)[...].astype(F32) + near[b].astype(F32) + into[b].astype(F32)
                ).astype(BF16)

        half = X_ROWS // 2
        lo, hi = pl.ds(0, half), pl.ds(half, half)

        def second_start(me, held, into, right, left):
            far = turn(me, 2, 4)
            return [
                send(held.at[far, lo], into.at[0, lo], right),
                send(held.at[far, hi], into.at[0, hi], left),
                send(held.at[turn(me, 1, 4), hi], into.at[1, hi], right),
                send(held.at[turn(me, 3, 4), lo], into.at[1, lo], left),
            ]

        def second_relay(me, held, into, kept, copies, right, left):
            copies[0].wait_recv()
            kept[lo, :] = total2(into[0, lo, :], held[turn(me, 1, 4), lo, :])
            one = send(kept.at[lo], into.at[2, lo], right)
            copies[1].wait_recv()
            kept[hi, :] = total2(into[0, hi, :], held[turn(me, 3, 4), hi, :])
            return [one, send(kept.at[hi], into.at[2, hi], left)]

        def second_finish(me, held, into, copies, offset):
            arrived(copies)
            total = (held[me].astype(F32) + into[1].astype(F32) + into[2].astype(F32)).astype(BF16)
            for u in range(UNITS):
                for hf in range(2):
                    last_out[2 * u + hf, offset : offset + half, :] = total[
                        hf * half : (hf + 1) * half, u * HD : (u + 1) * HD
                    ]

        def start():
            x_far_sends = far_sends(x, x_src, xa, x_right, x_left)
            y_far_sends = far_sends(y, y_src, ya, y_right, y_left)
            x_near = near_sends(x, x_src, xb, x_right, x_left)
            y_near = near_sends(y, y_src, yb, y_right, y_left)
            for u in range(UNITS):
                for hf in range(2):
                    for a in range(8):
                        top = a * BLOCK_ROWS + 4 * X_ROWS + Z_ROWS * hf
                        tz[2 * u + hf, a] = t[top : top + Z_ROWS, u * HD : (u + 1) * HD]
            z_sends = [send(tz.at[turn(z, k, 8)], zr.at[k - 1], z_peers[k]) for k in z_order]
            yield
            x_relays = relay(x, x_src, xa, xm, xc, x_far_sends, x_right, x_left)
            y_relays = relay(y, y_src, ya, ym, yc, y_far_sends, y_right, y_left)
            yield
            finish(x, x_src, xb, xc, x_near + x_relays, xu)
            x_second = second_start(y, xu, x2, y_right, y_left)
            finish(y, y_src, yb, yc, y_near + y_relays, yu)
            y_second = second_start(x, yu, y2, x_right, x_left)
            arrived(z_sends)
            total = tz[z].astype(F32)
            for k in range(7):
                total = total + zr[k].astype(F32)
            zu[...] = total.astype(BF16)

            def quad(x_lo_at):
                return pl.ds(pl.multiple_of(x_lo_at * 4, 4), 4)

            z_first = [
                send(zu.at[quad(x_lo)], zx.at[0], x_far),
                send(zu.at[quad(1 - x_lo)], zx.at[1], x_right),
                send(zu.at[quad(1 - x_lo)], zx.at[2], x_left),
            ]
            yield
            x_more = second_relay(y, xu, x2, x2m, x_second, y_right, y_left)
            y_more = second_relay(x, yu, y2, y2m, y_second, x_right, x_left)
            arrived(z_first)
            total = zu[quad(x_lo)].astype(F32)
            for n in range(3):
                total = total + zx[n].astype(F32)
            zx[3] = total.astype(BF16)
            z_second = [
                send(zx.at[3, turn(y, 2, 4)], zy.at[0], y_far),
                send(zx.at[3, turn(y, 1, 4)], zy.at[1], y_right),
                send(zx.at[3, turn(y, 3, 4)], zy.at[2], y_left),
            ]
            yield
            second_finish(y, xu, x2, x_second[2:] + x_more, 0)
            second_finish(x, yu, y2, y_second[2:] + y_more, half)
            last = [send(last_out.at[turn(z, k, 8)], last_in.at[k - 1], z_peers[k]) for k in z_order]
            arrived(z_second)
            z_total = zx[3, y].astype(F32)
            for n in range(3):
                z_total = z_total + zy[n].astype(F32)
            yield
            arrived(last)
            total = last_out[z].astype(F32)
            for k in range(7):
                total = total + last_in[k].astype(F32)
            yield jnp.concatenate([total, z_total], axis=0).astype(BF16)

        return start()

    def weight_sums(t, ht, gt, mine, sib_ht, sib_gt, theirs):
        head_qkv, head_att = pl.ds(0, 3 * HD), pl.ds(3 * HD, HD)

        def body(i, carry):
            at = pl.ds(pl.multiple_of(i * BLOCK_ROWS, BLOCK_ROWS), BLOCK_ROWS)
            t[at, head_qkv] = (
                nn(ht[at, :], mine[core, :, head_qkv]) + nn(sib_ht[at, :], theirs[:, head_qkv])
            ).astype(BF16)
            t[at, head_att] = (
                nn(gt[at, :], mine[core, :, head_att]) + nn(sib_gt[at, :], theirs[:, head_att])
            ).astype(BF16)
            return carry

        lax.fori_loop(0, features // BLOCK_ROWS, body, 0)

    def gather_heads(src):
        for n in range(3):
            for h in range(HEADS):
                dp[:, (2 * n + h) * HD : (2 * n + h + 1) * HD] = src[h, :, n * HD : (n + 1) * HD]

    gather_heads(back)

    def input_back(weight):
        def body(at):
            acc[:, at] = nt(dp[...], weight[at, :])

        by_columns(body)

    input_back(w1)
    t1, t0 = boxes[1][0], boxes[0][0]
    arrived(shared1)
    weight_sums(t1, ht1, gt1, back, sib_ht1, sib_gt1, sib_b1)
    steps1 = reduction(boxes[1], t1)
    next(steps1)

    def temporal_back(at):
        normed, inv_std = normalize(mid[at, :].astype(F32))
        term = norm_back(acc[at, :] * (1.0 + mod(scale1)), normed, inv_std)
        d_mid = (cot_ref[at, :].astype(F32) + term).astype(BF16)
        mid[at, :] = d_mid
        g0[at, :] = (mod(gate0) * d_mid.astype(F32)).astype(BF16)

    by_rows(temporal_back)

    flip(g0, gt0)
    shared0.append(send(gt0, sib_gt0, sibling))
    d_att0 = nt(g0[...], wo0[...]).astype(BF16)
    for h in range(HEADS):
        grads = attend_back(part(0, h), part(1, h), part(2, h), probs[h], d_att0[:, h * HD : (h + 1) * HD])
        for n, part_of in enumerate(grads):
            b0[h, :, n * HD : (n + 1) * HD] = part_of
    shared0.append(send(b0.at[1 - core], sib_b0, sibling))
    next(steps1)
    gather_heads(b0)
    arrived(shared0)
    weight_sums(t0, ht0, gt0, b0, sib_ht0, sib_gt0, sib_b0)
    steps0 = reduction(boxes[0], t0)
    next(steps0)
    next(steps1)
    input_back(w0)

    def spatial_back(at):
        normed, inv_std = normalize(x_ref[at, :].astype(F32))
        term = norm_back(acc[at, :] * (1.0 + mod(scale0)), normed, inv_std)
        grad_ref[at, :] = (mid[at, :].astype(F32) + term).astype(BF16)

    next(steps0)
    next(steps1)
    by_rows(spatial_back)
    next(steps0)
    next(steps1)
    next(steps0)
    total1 = next(steps1)
    next(steps0)
    total0 = next(steps0)

    slots, held_rows = 8 * 4 * SLOT, 2 * (X_ROWS // 2) + Z_ROWS
    half = X_ROWS // 2
    hf = lax.rem(z, 2)
    slot = lax.broadcasted_iota(jnp.int32, (slots, held_rows), 0)
    at = lax.broadcasted_iota(jnp.int32, (slots, held_rows), 1)
    edge = X_ROWS * x_hi + half * hf
    turn_of = lax.bitwise_and(lax.shift_right_logical(at, 3), 1)
    last_rows = jnp.where(turn_of == x_hi, at - 2 * half + 4 * X_ROWS + Z_ROWS * hf, -1)
    have = jnp.where(at < half, at + edge, jnp.where(at < 2 * half, at - half + 2 * X_ROWS + edge, last_rows))
    within = lax.bitwise_and(slot, SLOT - 1)
    want = lax.shift_right_logical(slot, 4) * OWN + within
    pick = jnp.where((have == want) & (within < OWN), 1.0, 0.0).astype(BF16)
    for b, total in enumerate((total0, total1)):
        spread[:, b] = nn(pick, total).astype(BF16).reshape(8, 4 * SLOT, HD)
    gathers = [send(spread.at[turn(z, k, 8)], gather.at[z], z_peers[k]) for k in z_order]
    gather[z] = spread[z]
    arrived(gathers)
    for u in range(UNITS):
        both = (gather[2 * u].astype(F32) + gather[2 * u + 1].astype(F32)).astype(BF16)
        for b in range(2):
            for n in range(4):
                merged[n, b, u] = both[b, n * SLOT : (n + 1) * SLOT, :]
    finals = [
        send(merged.at[mate_core * 2 + mate_hi], final.at[n], mates[n])
        for n, (mate_core, mate_hi) in enumerate([(1 - core, x_hi), (core, 1 - x_hi), (1 - core, 1 - x_hi)])
    ]
    arrived(finals)
    sums_ref[core] = merged[core * 2 + x_hi].astype(F32) + final[1].astype(F32)
    sums_ref[1 - core] = final[0].astype(F32) + final[2].astype(F32)
    for copy in used:
        copy.wait_send()


def whole(tokens, ids, cotangent, modulation, w_qkv, w_out):
    _, rows, features = tokens.shape
    inner = HEADS * HD

    def vmem(*shape, dtype=BF16):
        return pltpu.VMEM(shape, dtype)

    full = lambda: vmem(rows, features)
    flipped = lambda: vmem(features, rows)
    ring = [vmem(4, X_ROWS, WIDE) for _ in range(5)]
    second = [vmem(3, X_ROWS, WIDE), vmem(X_ROWS, WIDE)]
    reduction = (
        [vmem(features, WIDE)] + ring + ring + second + second + [
            vmem(8, 8, Z_ROWS, HD), vmem(7, 8, Z_ROWS, HD), vmem(8, Z_ROWS, HD),
            vmem(4, 4, Z_ROWS, HD), vmem(3, Z_ROWS, HD),
            vmem(8, X_ROWS, HD), vmem(7, X_ROWS, HD),
        ]
    )
    scratch = [
        full(), full(), vmem(features, 3 * inner), vmem(features, 3 * inner),
        vmem(inner, features), vmem(inner, features),
        full(), full(), full(), full(), full(), vmem(rows, features, dtype=F32),
        vmem(rows, 3 * inner), vmem(HEADS, rows, rows, dtype=F32), vmem(rows, inner),
    ] + [flipped() for _ in range(8)] + [
        vmem(HEADS, rows, WIDE), vmem(HEADS, FRAMES, rows // FRAMES, WIDE),
        vmem(HEADS, rows, WIDE), vmem(HEADS, rows, WIDE),
        vmem(rows, 3 * inner), vmem(HEADS, rows, WIDE), vmem(rows, WIDE), vmem(rows, WIDE),
    ] + reduction + reduction + [
        vmem(8, 2, 4 * SLOT, HD), vmem(8, 2, 4 * SLOT, HD),
        vmem(4, 2, UNITS, SLOT, HD), vmem(3, 2, UNITS, SLOT, HD),
        pltpu.SemaphoreType.DMA((6,)),
        pltpu.SemaphoreType.DMA((160,)),
        pltpu.SemaphoreType.DMA((160,)),
    ]
    in_vmem = pl.BlockSpec(memory_space=pltpu.VMEM)
    anywhere = pl.BlockSpec(memory_space=pl.ANY)
    return pl.pallas_call(
        whole_kernel,
        out_shape=(
            jax.ShapeDtypeStruct((rows, features), BF16),
            jax.ShapeDtypeStruct((2, 2, UNITS, SLOT, HD), F32),
        ),
        in_specs=[anywhere, in_vmem, anywhere, in_vmem, anywhere, anywhere],
        out_specs=(in_vmem, in_vmem),
        scratch_shapes=scratch,
        compiler_params=pltpu.CompilerParams(
            collective_id=0, has_side_effects=True, vmem_limit_bytes=60 * 2**20
        ),
    )(tokens, ids, cotangent, modulation, w_qkv, w_out)


def local(tokens, window_ids, cotangent, modulation, w_qkv, w_out):
    rows = tokens.shape[1]
    d_tokens, sums = whole(tokens, window_ids, cotangent, modulation, w_qkv, w_out)
    factor = 1.0 / math.sqrt(rows * lax.axis_size("seq") * lax.axis_size("rep"))
    sums = (sums[:, :, :, :OWN] * factor).astype(BF16)
    grad_qkv = sums[:, :, :3].transpose(1, 3, 2, 0, 4).reshape(2, OWN, 3 * HEADS * HD)
    grad_out = sums[:, :, 3].transpose(1, 0, 3, 2).reshape(2, HEADS * HD, OWN)
    return (d_tokens[None], grad_qkv, grad_out)


def solution(mesh):
    in_specs = (P("rep", "seq", None), P("rep", "seq"), P("rep", "seq", None), P(), P(), P())
    out_specs = (
        P("rep", "seq", None),
        P(None, ("seq", "rep"), None),
        P(None, None, ("seq", "rep")),
    )
    return jax.shard_map(local, mesh=mesh, in_specs=in_specs, out_specs=out_specs, check_vma=False)
```

```python
import math

import jax
import jax.numpy as jnp
from jax import lax
from jax.experimental import pallas as pl
from jax.experimental.pallas import tpu as pltpu
from jax.sharding import PartitionSpec as P

MESH = pl.DeviceIdType.MESH
BF16, F32 = jnp.bfloat16, jnp.float32
HD = 128
HEADS = 2
FRAMES = 8
UNITS = 4
WIDE = UNITS * HD
BLOCK_ROWS = 288
X_ROWS, Z_ROWS = 64, 16
OWN = 9
SLOT = 16
epsilon = 1e-06
factor_of_scores = HD ** (-0.5)


def nn(left, right):
    return lax.dot_general(left, right, (((1,), (0,)), ((), ())), preferred_element_type=F32)


def nt(left, right):
    return lax.dot_general(left, right, (((1,), (1,)), ((), ())), preferred_element_type=F32)


def softmax(query, key, mask):
    scores = jnp.where(mask, nt(query, key) * factor_of_scores, -1e30)
    expd = jnp.exp(scores - jnp.max(scores, axis=-1, keepdims=True))
    return expd / jnp.sum(expd, axis=-1, keepdims=True)


def attend_back(query, key, value, probs, d_out):
    d_value = nn(probs.astype(BF16).T, d_out)
    d_prob = nt(d_out, value)
    d_score = (probs * (d_prob - jnp.sum(probs * d_prob, axis=-1, keepdims=True))).astype(BF16)
    d_query = nn(d_score, key) * factor_of_scores
    d_key = nn(d_score.T, query) * factor_of_scores
    return d_query.astype(BF16), d_key.astype(BF16), d_value.astype(BF16)


def normalize(values):
    centered = values - jnp.mean(values, axis=-1, keepdims=True)
    inv_std = lax.rsqrt(jnp.mean(centered * centered, axis=-1, keepdims=True) + epsilon)
    return centered * inv_std, inv_std


def norm_back(d_normed, normed, inv_std):
    return inv_std * (
        d_normed
        - jnp.mean(d_normed, axis=-1, keepdims=True)
        - normed * jnp.mean(d_normed * normed, axis=-1, keepdims=True)
    )


def whole_kernel(tokens_hbm, ids_ref, cot_hbm, mod_ref, qkv_hbm, out_hbm,
                 grad_hbm, qkv_ref, att_ref,
                 x_ref, cot_ref, w0, w1, wo0, wo1,
                 hid0, hid1, mid, g1, g0, acc, pk0, probs, att0,
                 left0, left1, out_s, in_s, out_p, back, b0, sib_b1, sib_b0,
                 *rest):
    per_block = 20
    boxes = [rest[:per_block], rest[per_block : 2 * per_block]]
    held, gather, merged, final, load_sem, send_sem, recv_sem = rest[2 * per_block :]

    seq = lax.axis_index("seq")
    x_hi = lax.axis_index("rep")
    core = lax.rem(seq, 2)
    z = lax.rem(lax.div(seq, 2), 8)
    y = lax.rem(lax.div(seq, 16), 4)
    x_lo = lax.div(seq, 64)
    x = 2 * x_hi + x_lo
    frame = x_lo * 4 + y

    loads = []
    for n, (src, dst) in enumerate([
        (tokens_hbm.at[0], x_ref), (qkv_hbm.at[0], w0), (out_hbm.at[0], wo0),
        (cot_hbm.at[0], cot_ref), (out_hbm.at[1], wo1), (qkv_hbm.at[1], w1),
    ]):
        loads.append(pltpu.make_async_copy(src, dst, load_sem.at[n]))
        loads[n].start()

    def device(x_at, y_at, z_at, core_at):
        return {"seq": ((lax.rem(x_at, 2) * 4 + y_at) * 8 + z_at) * 2 + core_at, "rep": lax.div(x_at, 2)}

    def turn(at, step, size):
        return lax.rem(at + step, size)

    x_right, x_left = device(turn(x, 1, 4), y, z, core), device(turn(x, 3, 4), y, z, core)
    x_far_at = turn(x, 2, 4)
    z_order = (4, 3, 5, 2, 6, 1, 7)
    z_peers = {k: device(x, y, turn(z, k, 8), core) for k in z_order}
    mates = [device(x, y, z, 1 - core), device(x_far_at, y, z, core), device(x_far_at, y, z, 1 - core)]
    sibling, x_far = mates[0], mates[1]
    other = 2 * x_hi + 1 - x_lo
    clip = []
    for cross, step in ((1, 2), (1, 1), (1, 3), (1, 0), (0, 2), (0, 1), (0, 3)):
        y_at = turn(y, step, 4)
        frame_at = (1 - x_lo if cross else x_lo) * 4 + y_at
        clip.append((frame_at, device(other if cross else x, y_at, z, core)))
    y_far, y_right, y_left = clip[4][1], clip[5][1], clip[6][1]

    x_ring = ((2, x_far), (1, x_right), (3, x_left))
    y_ring = ((2, y_far), (1, y_right), (3, y_left))

    barrier = pltpu.get_barrier_semaphore()
    peers = [x_right, x_left] + mates + list(z_peers.values()) + [peer for _, peer in clip]
    for peer in peers:
        pl.semaphore_signal(barrier, inc=1, device_id=peer, device_id_type=MESH)

    used = []

    def send(src, dst, peer):
        at = len(used)
        copy = pltpu.make_async_remote_copy(
            src_ref=src, dst_ref=dst, send_sem=send_sem.at[at], recv_sem=recv_sem.at[at],
            device_id=peer, device_id_type=MESH,
        )
        copy.start()
        used.append(copy)
        return copy

    def arrived(copies):
        for copy in copies:
            copy.wait_recv()

    rows_of = x_ref.shape[0]
    features = x_ref.shape[1]
    shift0, scale0, gate0, shift1, scale1, gate1 = range(6)

    def mod(n):
        return mod_ref[n : n + 1, :]

    def by_rows(body):
        def step(i, carry):
            body(pl.ds(pl.multiple_of(i * 16, 16), 16))
            return carry

        lax.fori_loop(0, rows_of // 16, step, 0, unroll=8)

    def by_columns(body, size=1152):
        def step(i, carry):
            body(pl.ds(pl.multiple_of(i * size, size), size))
            return carry

        lax.fori_loop(0, features // size, step, 0)

    loads[0].wait()

    def spatial_in(at):
        normed, _ = normalize(x_ref[at, :].astype(F32))
        hid0[at, :] = (normed * (1.0 + mod(scale0)) + mod(shift0)).astype(BF16)

    by_rows(spatial_in)
    loads[1].wait()

    def project0(i, carry):
        at = pl.ds(pl.multiple_of(i * 256, 256), 256)
        pk0[:, at] = nn(hid0[...], w0[:, at]).astype(BF16)
        return carry

    lax.fori_loop(0, 3, project0, 0)

    ids = jnp.broadcast_to(ids_ref[...], (rows_of, rows_of))
    mask = ids == ids.T

    def part(n, h):
        return pk0[:, (2 * n + h) * HD : (2 * n + h + 1) * HD]

    for h in range(HEADS):
        p = softmax(part(0, h), part(1, h), mask)
        probs[h] = p
        att = nn(p.astype(BF16), part(2, h)).astype(BF16)
        att0[:, h * HD : (h + 1) * HD] = att
        b0[h, 3] = att
    loads[2].wait()

    def middle(at):
        mid[:, at] = (
            x_ref[:, at].astype(F32) + mod_ref[gate0 : gate0 + 1, at] * nn(att0[...], wo0[:, at])
        ).astype(BF16)

    by_columns(middle)

    def temporal_in(at):
        normed, _ = normalize(mid[at, :].astype(F32))
        hid1[at, :] = (normed * (1.0 + mod(scale1)) + mod(shift1)).astype(BF16)

    by_rows(temporal_in)
    loads[3].wait()

    def gate_top(at):
        g1[at, :] = (mod(gate1) * cot_ref[at, :].astype(F32)).astype(BF16)

    by_rows(gate_top)
    loads[4].wait()
    d_att1 = nt(g1[...], wo1[...]).astype(BF16)
    for h in range(HEADS):
        out_s[h, 3] = d_att1[:, h * HD : (h + 1) * HD]

    pixels = rows_of // FRAMES

    def pixel_rows(n):
        return pl.ds(pl.multiple_of(n * pixels, pixels), pixels)

    mine_rows, heads, first_kinds = pixel_rows(frame), pl.ds(0, HEADS), pl.ds(0, 3)
    pl.semaphore_wait(barrier, len(peers))
    gone_d = [
        send(out_s.at[heads, 3, pixel_rows(at)], in_s.at[heads, 3, mine_rows], peer) for at, peer in clip
    ]
    loads[5].wait()
    packed = nn(hid1[...], w1[...]).astype(BF16)
    for n in range(3):
        for h in range(HEADS):
            out_s[h, n] = packed[:, (2 * n + h) * HD : (2 * n + h + 1) * HD]
    gone = [
        [
            send(out_s.at[h, first_kinds, pixel_rows(at)], in_s.at[h, first_kinds, mine_rows], peer)
            for at, peer in clip
        ]
        for h in range(HEADS)
    ]

    order = (0, 4, 1, 5, 2, 6, 3, 7, 8, 12, 9, 13, 10, 14, 11, 15, 16, 17)
    own_tokens, sib_tokens = pl.ds(0, rows_of), pl.ds(rows_of, rows_of)

    def flip(src, dst, n):
        size = 4 * BLOCK_ROWS
        for top in range(0, features, size):
            turned = src[:, top : top + size].T
            for block in range(0, size, BLOCK_ROWS):
                for at, tile in enumerate(order):
                    dst[n, top + block + at * 16 : top + block + at * 16 + 16, 0:rows_of] = turned[
                        block + tile * 16 : block + tile * 16 + 16, :
                    ]
        return send(dst.at[n, :, own_tokens], dst.at[n, :, sib_tokens], sibling)

    shared1 = [flip(hid1, left1, 0), flip(g1, left1, 1)]

    pixel_row = lax.bitwise_and(lax.broadcasted_iota(jnp.int32, (rows_of, rows_of), 0), pixels - 1)
    pixel_col = lax.bitwise_and(lax.broadcasted_iota(jnp.int32, (rows_of, rows_of), 1), pixels - 1)
    same_pixel = pixel_row == pixel_col
    came = []
    arrived(gone_d)
    for h in range(HEADS):
        in_s[h, :, mine_rows, :] = out_s[h, :, mine_rows, :]
        arrived(gone[h])
        query, key, value, d_out = [in_s[h, n] for n in range(UNITS)]
        p = softmax(query, key, same_pixel)
        out_p[h, 3] = nn(p.astype(BF16), value).astype(BF16)
        for n, part_of in enumerate(attend_back(query, key, value, p, d_out)):
            out_p[h, n] = part_of
        came.append([
            send(out_p.at[h, :, pixel_rows(at)], back.at[h, :, mine_rows], peer) for at, peer in clip
        ])
    shared0 = [flip(hid0, left0, 0)]
    for h in range(HEADS):
        back[h, :, mine_rows, :] = out_p[h, :, mine_rows, :]
        arrived(came[h])
    kinds = pl.ds(pl.multiple_of(2 * core, 2), 2)
    sib_kinds = pl.ds(pl.multiple_of(2 * (1 - core), 2), 2)
    shared1.append(send(back.at[heads, sib_kinds], sib_b1, sibling))

    def reduction(box, t, b):
        (_, xa, xc, xm, xb, xu, ya, yc, ym, yb, yu, x2, y2, tz, zr, zu, zx, zy, last_out, last_in) = box

        def rows(x_at, y_at, offset):
            start = (lax.rem(x_at, 2) * 4 + y_at) * BLOCK_ROWS + offset + X_ROWS * lax.div(x_at, 2)
            return pl.ds(pl.multiple_of(start, 16), X_ROWS)

        def x_src(a, b):
            return t.at[rows(a, b, 0)]

        def y_src(a, b):
            return t.at[rows(b, a, 2 * X_ROWS)]

        def total2(one, two):
            return (one.astype(F32) + two.astype(F32)).astype(BF16)

        def far_sends(me, src, into, right, left):
            far = turn(me, 2, 4)
            return (
                [send(src(far, b), into.at[b], right) for b in (0, 1)]
                + [send(src(far, b), into.at[b], left) for b in (2, 3)]
            )

        def near_sends(me, src, into, right, left):
            return (
                [send(src(turn(me, 1, 4), b), into.at[b], right) for b in (2, 3)]
                + [send(src(turn(me, 3, 4), b), into.at[b], left) for b in (0, 1)]
            )

        def relay(me, src, box_in, kept, into, far, right, left):
            outs = []
            for n in (0, 2, 1, 3):
                far[n].wait_recv()
                kept[n] = total2(box_in[n], src(turn(me, 1 if n < 2 else 3, 4), n)[...])
                outs.append(send(kept.at[n], into.at[n], right if n < 2 else left))
            return outs

        def finish(me, src, near, into, copies, result):
            arrived(copies)
            for b in range(4):
                result[b] = (
                    src(me, b)[...].astype(F32) + near[b].astype(F32) + into[b].astype(F32)
                ).astype(BF16)

        half = X_ROWS // 2

        def second_start(me, kept, into, ring):
            return [send(kept.at[turn(me, k, 4)], into.at[n], peer) for n, (k, peer) in enumerate(ring)]

        def second_finish(me, kept, into, copies, offset):
            arrived(copies)
            total = kept[me].astype(F32)
            for n in range(3):
                total = total + into[n].astype(F32)
            total = total.astype(BF16)
            for u in range(UNITS):
                for hf in range(2):
                    last_out[2 * u + hf, offset : offset + half, :] = total[
                        hf * half : (hf + 1) * half, u * HD : (u + 1) * HD
                    ]

        def start():
            x_far_sends = far_sends(x, x_src, xa, x_right, x_left)
            y_far_sends = far_sends(y, y_src, ya, y_right, y_left)
            x_near = near_sends(x, x_src, xb, x_right, x_left)
            y_near = near_sends(y, y_src, yb, y_right, y_left)
            for u in range(UNITS):
                for hf in range(2):
                    for a in range(8):
                        top = a * BLOCK_ROWS + 4 * X_ROWS + Z_ROWS * hf
                        tz[2 * u + hf, a] = t[top : top + Z_ROWS, u * HD : (u + 1) * HD]
            z_sends = [send(tz.at[turn(z, k, 8)], zr.at[k - 1], z_peers[k]) for k in z_order]
            yield
            x_relays = relay(x, x_src, xa, xm, xc, x_far_sends, x_right, x_left)
            y_relays = relay(y, y_src, ya, ym, yc, y_far_sends, y_right, y_left)
            yield
            finish(x, x_src, xb, xc, x_near + x_relays, xu)
            x_second = second_start(y, xu, x2, y_ring)
            finish(y, y_src, yb, yc, y_near + y_relays, yu)
            y_second = second_start(x, yu, y2, x_ring)
            arrived(z_sends)
            total = tz[z].astype(F32)
            for k in range(7):
                total = total + zr[k].astype(F32)
            zu[...] = total.astype(BF16)

            def quad(x_lo_at):
                return pl.ds(pl.multiple_of(x_lo_at * 4, 4), 4)

            z_first = [
                send(zu.at[quad(x_lo)], zx.at[0], x_far),
                send(zu.at[quad(1 - x_lo)], zx.at[1], x_right),
                send(zu.at[quad(1 - x_lo)], zx.at[2], x_left),
            ]
            yield
            second_finish(y, xu, x2, x_second, 0)
            second_finish(x, yu, y2, y_second, half)
            last = [send(last_out.at[turn(z, k, 8)], last_in.at[k - 1], z_peers[k]) for k in z_order]
            arrived(z_first)
            total = zu[quad(x_lo)].astype(F32)
            for n in range(3):
                total = total + zx[n].astype(F32)
            zx[3] = total.astype(BF16)
            z_second = [send(zx.at[3, turn(y, k, 4)], zy.at[n], peer) for n, (k, peer) in enumerate(y_ring)]
            yield
            arrived(last)
            total = last_out[z].astype(F32)
            for k in range(7):
                total = total + last_in[k].astype(F32)
            for k in range(4):
                held[k, b] = total[k * SLOT : (k + 1) * SLOT, :].astype(BF16)
            arrived(z_second)
            total = zx[3, y].astype(F32)
            for n in range(3):
                total = total + zy[n].astype(F32)
            held[4, b] = total.astype(BF16)
            yield

        return start()

    def weight_sums(t, left, own, theirs):
        for n in range(2):
            right = jnp.concatenate(
                [
                    jnp.concatenate([own[h, 2 * core + n] for h in range(HEADS)], axis=1),
                    jnp.concatenate([theirs[h, n] for h in range(HEADS)], axis=1),
                ],
                axis=0,
            )
            source = core if n == 1 else 0

            def body(at):
                t[at, 2 * n * HD : 2 * (n + 1) * HD] = nn(left[source, at, :], right).astype(BF16)

            by_columns(body)

    def input_back(src, weight):
        d_packed = jnp.concatenate([src[h, n] for n in range(3) for h in range(HEADS)], axis=1)

        def body(at):
            acc[:, at] = nt(d_packed, weight[at, :])

        by_columns(body)

    input_back(back, w1)
    t1, t0 = boxes[1][0], boxes[0][0]
    arrived(shared1)
    weight_sums(t1, left1, back, sib_b1)
    steps1 = reduction(boxes[1], t1, 1)
    next(steps1)

    def temporal_back(at):
        normed, inv_std = normalize(mid[at, :].astype(F32))
        term = norm_back(acc[at, :] * (1.0 + mod(scale1)), normed, inv_std)
        d_mid = (cot_ref[at, :].astype(F32) + term).astype(BF16)
        mid[at, :] = d_mid
        g0[at, :] = (mod(gate0) * d_mid.astype(F32)).astype(BF16)

    by_rows(temporal_back)

    shared0.append(flip(g0, left0, 1))
    d_att0 = nt(g0[...], wo0[...]).astype(BF16)
    for h in range(HEADS):
        grads = attend_back(part(0, h), part(1, h), part(2, h), probs[h], d_att0[:, h * HD : (h + 1) * HD])
        for n, part_of in enumerate(grads):
            b0[h, n] = part_of
    shared0.append(send(b0.at[heads, sib_kinds], sib_b0, sibling))
    next(steps1)
    input_back(b0, w0)
    arrived(shared0)
    weight_sums(t0, left0, b0, sib_b0)
    steps0 = reduction(boxes[0], t0, 0)
    next(steps0)
    next(steps1)

    def spatial_back(at):
        normed, inv_std = normalize(x_ref[at, :].astype(F32))
        term = norm_back(acc[at, :] * (1.0 + mod(scale0)), normed, inv_std)
        mid[at, :] = (mid[at, :].astype(F32) + term).astype(BF16)

    by_rows(spatial_back)
    store = pltpu.make_async_copy(mid, grad_hbm, load_sem.at[0])
    store.start()
    next(steps0)
    next(steps1)
    next(steps0)
    next(steps1)
    next(steps0)
    next(steps0)

    def tile_for(z_at, group):
        most = 4 - x_hi
        ahead = lax.max(36 * z_at + 35 - SLOT * group, 0)
        return lax.min(lax.div(ahead, 4 * SLOT), most)

    group = 2 * x_hi + lax.rem(z, 2)
    gathers = [
        send(held.at[tile_for(turn(z, k, 8), group)], gather.at[z], z_peers[k]) for k in z_order
    ]
    gather[z] = held[tile_for(z, group)]
    slot = lax.broadcasted_iota(jnp.int32, (4 * SLOT, 2 * SLOT), 0)
    at = lax.broadcasted_iota(jnp.int32, (4 * SLOT, 2 * SLOT), 1)
    tops = [4 * SLOT * tile_for(z, 2 * x_hi + hf) + SLOT * (2 * x_hi + hf) - 36 * z for hf in range(2)]
    have = jnp.where(at < SLOT, at + tops[0], at - SLOT + tops[1])
    within = lax.bitwise_and(slot, SLOT - 1)
    want = lax.shift_right_logical(slot, 4) * OWN + within
    pick = jnp.where((have == want) & (within < OWN), 1.0, 0.0).astype(BF16)
    arrived(gathers)
    tiles = jnp.concatenate(
        [
            jnp.concatenate([gather[2 * u + hf, b] for b in range(2) for u in range(UNITS)], axis=1)
            for hf in range(2)
        ],
        axis=0,
    )
    owned = nn(pick, tiles).astype(BF16)
    for n in range(4):
        for b in range(2):
            for u in range(UNITS):
                lanes = (b * UNITS + u) * HD
                merged[n, b, u] = owned[n * SLOT : (n + 1) * SLOT, lanes : lanes + HD]
    finals = [
        send(merged.at[mate_core * 2 + mate_hi], final.at[n], mates[n])
        for n, (mate_core, mate_hi) in enumerate([(1 - core, x_hi), (core, 1 - x_hi), (1 - core, 1 - x_hi)])
    ]
    arrived(finals)
    scale = 1.0 / math.sqrt(rows_of * lax.axis_size("seq") * lax.axis_size("rep"))
    same = (merged[core * 2 + x_hi].astype(F32) + final[1].astype(F32)) * scale
    others = (final[0].astype(F32) + final[2].astype(F32)) * scale
    cores = [jnp.where(core == 0, same, others), jnp.where(core == 0, others, same)]
    for b in range(2):
        for c in range(2):
            for u in range(UNITS):
                unit = cores[c][b, u]
                n = c * UNITS + u
                into, lanes = (qkv_ref, n * HD) if n < 6 else (att_ref, (n - 6) * HD)
                for i in range(OWN):
                    into[i, b : b + 1, lanes : lanes + HD] = unit[i : i + 1, :]
    store.wait()
    for copy in used:
        copy.wait_send()


def whole(tokens, ids, cotangent, modulation, w_qkv, w_out):
    _, rows, features = tokens.shape
    inner = HEADS * HD

    def vmem(*shape, dtype=BF16):
        return pltpu.VMEM(shape, dtype)

    full = lambda: vmem(rows, features)
    pooled = lambda: vmem(2, features, 2 * rows)
    units = lambda: vmem(HEADS, UNITS, rows, HD)
    ring = [vmem(4, X_ROWS, WIDE) for _ in range(5)]
    second = [vmem(3, X_ROWS, WIDE)]
    reduction = (
        [vmem(features, WIDE)] + ring + ring + second + second + [
            vmem(8, 8, Z_ROWS, HD), vmem(7, 8, Z_ROWS, HD), vmem(8, Z_ROWS, HD),
            vmem(4, 4, Z_ROWS, HD), vmem(3, Z_ROWS, HD),
            vmem(8, X_ROWS, HD), vmem(7, X_ROWS, HD),
        ]
    )
    scratch = [
        full(), full(), vmem(features, 3 * inner), vmem(features, 3 * inner),
        vmem(inner, features), vmem(inner, features),
        full(), full(), full(), full(), full(), vmem(rows, features, dtype=F32),
        vmem(rows, 3 * inner), vmem(HEADS, rows, rows, dtype=F32), vmem(rows, inner),
    ] + [pooled(), pooled()] + [units() for _ in range(5)] + [
        vmem(HEADS, 2, rows, HD), vmem(HEADS, 2, rows, HD),
    ] + reduction + reduction + [
        vmem(5, 2, SLOT, HD), vmem(8, 2, SLOT, HD),
        vmem(4, 2, UNITS, SLOT, HD), vmem(3, 2, UNITS, SLOT, HD),
        pltpu.SemaphoreType.DMA((6,)),
        pltpu.SemaphoreType.DMA((160,)),
        pltpu.SemaphoreType.DMA((160,)),
    ]
    in_vmem = pl.BlockSpec(memory_space=pltpu.VMEM)
    anywhere = pl.BlockSpec(memory_space=pl.ANY)
    return pl.pallas_call(
        whole_kernel,
        out_shape=(
            jax.ShapeDtypeStruct((rows, features), BF16),
            jax.ShapeDtypeStruct((OWN, 2, 3 * inner), F32),
            jax.ShapeDtypeStruct((OWN, 2, inner), F32),
        ),
        in_specs=[anywhere, in_vmem, anywhere, in_vmem, anywhere, anywhere],
        out_specs=(anywhere, in_vmem, in_vmem),
        scratch_shapes=scratch,
        compiler_params=pltpu.CompilerParams(
            collective_id=0, has_side_effects=True, vmem_limit_bytes=60 * 2**20
        ),
    )(tokens, ids, cotangent, modulation, w_qkv, w_out)


def hand_over_kernel(grad_hbm, qkv_ref, att_ref, tokens_out, qkv_out, att_out, sems):
    chunk = grad_hbm.shape[0] // 4
    copies = []
    for n in range(4):
        at = pl.ds(n * chunk, chunk)
        copies.append(pltpu.make_async_copy(grad_hbm.at[at], tokens_out.at[at], sems.at[n]))
        copies[n].start()
    qkv_out[...] = qkv_ref[...].astype(BF16)
    att_out[...] = att_ref[...].astype(BF16)
    for copy in copies:
        copy.wait()


def hand_over(grad, qkv, att):
    in_vmem = pl.BlockSpec(memory_space=pltpu.VMEM)
    anywhere = pl.BlockSpec(memory_space=pltpu.HBM)
    return pl.pallas_call(
        hand_over_kernel,
        out_shape=tuple(jax.ShapeDtypeStruct(a.shape, BF16) for a in (grad, qkv, att)),
        in_specs=[anywhere, in_vmem, in_vmem],
        out_specs=(anywhere, in_vmem, in_vmem),
        scratch_shapes=[pltpu.SemaphoreType.DMA((4,))],
    )(grad, qkv, att)


def local(tokens, window_ids, cotangent, modulation, w_qkv, w_out):
    d_tokens, qkv, out = hand_over(
        *whole(tokens, window_ids, cotangent, modulation, w_qkv, w_out)
    )
    return (d_tokens[None], qkv.transpose(1, 0, 2), out.transpose(1, 2, 0))


def solution(mesh):
    in_specs = (P("rep", "seq", None), P("rep", "seq"), P("rep", "seq", None), P(), P(), P())
    out_specs = (
        P("rep", "seq", None),
        P(None, ("seq", "rep"), None),
        P(None, None, ("seq", "rep")),
    )
    return jax.shard_map(local, mesh=mesh, in_specs=in_specs, out_specs=out_specs, check_vma=False)
```

```python
import math

import jax
import jax.numpy as jnp
from jax import lax
from jax.experimental import pallas as pl
from jax.experimental.pallas import tpu as pltpu
from jax.sharding import PartitionSpec as P

MESH = pl.DeviceIdType.MESH
BF16, F32 = jnp.bfloat16, jnp.float32
HD = 128
HEADS = 2
FRAMES = 8
UNITS = 4
WIDE = UNITS * HD
BLOCK_ROWS = 288
X_ROWS, Z_ROWS = 64, 16
OWN = 9
SLOT = 16
epsilon = 1e-06
factor_of_scores = HD ** (-0.5)


def nn(left, right):
    return lax.dot_general(left, right, (((1,), (0,)), ((), ())), preferred_element_type=F32)


def nt(left, right):
    return lax.dot_general(left, right, (((1,), (1,)), ((), ())), preferred_element_type=F32)


def softmax(query, key, mask):
    scores = jnp.where(mask, nt(query, key) * factor_of_scores, -1e30)
    expd = jnp.exp(scores - jnp.max(scores, axis=-1, keepdims=True))
    return expd / jnp.sum(expd, axis=-1, keepdims=True)


def attend_back(query, key, value, probs, d_out):
    d_value = nn(probs.astype(BF16).T, d_out)
    d_prob = nt(d_out, value)
    d_score = (probs * (d_prob - jnp.sum(probs * d_prob, axis=-1, keepdims=True))).astype(BF16)
    d_query = nn(d_score, key) * factor_of_scores
    d_key = nn(d_score.T, query) * factor_of_scores
    return d_query.astype(BF16), d_key.astype(BF16), d_value.astype(BF16)


def normalize(values):
    centered = values - jnp.mean(values, axis=-1, keepdims=True)
    inv_std = lax.rsqrt(jnp.mean(centered * centered, axis=-1, keepdims=True) + epsilon)
    return centered * inv_std, inv_std


def norm_back(d_normed, normed, inv_std):
    return inv_std * (
        d_normed
        - jnp.mean(d_normed, axis=-1, keepdims=True)
        - normed * jnp.mean(d_normed * normed, axis=-1, keepdims=True)
    )


def whole_kernel(tokens_hbm, ids_ref, cot_hbm, mod_ref, qkv_hbm, out_hbm,
                 grad_ref, qkv_ref, att_ref,
                 x_ref, cot_ref, w0, w1, wo0, wo1,
                 hid0, hid1, mid, g1, g0, acc, pk0, probs, att0,
                 left0, left1, out_s, in_s, out_p, back, b0, sib_b1, sib_b0,
                 *rest):
    per_block = 24
    boxes = [rest[:per_block], rest[per_block : 2 * per_block]]
    load_sem, send_sem, recv_sem = rest[2 * per_block :]

    seq = lax.axis_index("seq")
    x_hi = lax.axis_index("rep")
    core = lax.rem(seq, 2)
    z = lax.rem(lax.div(seq, 2), 8)
    y = lax.rem(lax.div(seq, 16), 4)
    x_lo = lax.div(seq, 64)
    x = 2 * x_hi + x_lo
    frame = x_lo * 4 + y

    loads = []
    for n, (src, dst) in enumerate([
        (tokens_hbm.at[0], x_ref), (qkv_hbm.at[0], w0), (out_hbm.at[0], wo0),
        (cot_hbm.at[0], cot_ref), (out_hbm.at[1], wo1), (qkv_hbm.at[1], w1),
    ]):
        loads.append(pltpu.make_async_copy(src, dst, load_sem.at[n]))
        loads[n].start()

    def device(x_at, y_at, z_at, core_at):
        return {"seq": ((lax.rem(x_at, 2) * 4 + y_at) * 8 + z_at) * 2 + core_at, "rep": lax.div(x_at, 2)}

    def turn(at, step, size):
        return lax.rem(at + step, size)

    x_right, x_left = device(turn(x, 1, 4), y, z, core), device(turn(x, 3, 4), y, z, core)
    x_far_at = turn(x, 2, 4)
    z_order = (4, 3, 5, 2, 6, 1, 7)
    z_peers = {k: device(x, y, turn(z, k, 8), core) for k in z_order}
    sibling, x_far = device(x, y, z, 1 - core), device(x_far_at, y, z, core)
    far_z_peers = {k: device(x_far_at, y, turn(z, k, 8), core) for k in z_order}
    other = 2 * x_hi + 1 - x_lo
    clip = []
    for cross, step in ((1, 2), (1, 1), (1, 3), (1, 0), (0, 2), (0, 1), (0, 3)):
        y_at = turn(y, step, 4)
        frame_at = (1 - x_lo if cross else x_lo) * 4 + y_at
        clip.append((frame_at, device(other if cross else x, y_at, z, core)))
    y_far, y_right, y_left = clip[4][1], clip[5][1], clip[6][1]

    x_ring = ((2, x_far), (1, x_right), (3, x_left))
    y_ring = ((2, y_far), (1, y_right), (3, y_left))

    barrier = pltpu.get_barrier_semaphore()
    peers = [x_right, x_left, sibling, x_far] + [peer for _, peer in clip]
    peers += list(z_peers.values()) + list(far_z_peers.values())
    for peer in peers:
        pl.semaphore_signal(barrier, inc=1, device_id=peer, device_id_type=MESH)

    used = []

    def send(src, dst, peer):
        at = len(used)
        copy = pltpu.make_async_remote_copy(
            src_ref=src, dst_ref=dst, send_sem=send_sem.at[at], recv_sem=recv_sem.at[at],
            device_id=peer, device_id_type=MESH,
        )
        copy.start()
        used.append(copy)
        return copy

    def arrived(copies):
        for copy in copies:
            copy.wait_recv()

    rows_of = x_ref.shape[0]
    features = x_ref.shape[1]
    shift0, scale0, gate0, shift1, scale1, gate1 = range(6)

    def mod(n):
        return mod_ref[n : n + 1, :]

    def by_rows(body):
        def step(i, carry):
            body(pl.ds(pl.multiple_of(i * 16, 16), 16))
            return carry

        lax.fori_loop(0, rows_of // 16, step, 0, unroll=8)

    def by_columns(body, size=1152):
        def step(i, carry):
            body(pl.ds(pl.multiple_of(i * size, size), size))
            return carry

        lax.fori_loop(0, features // size, step, 0)

    loads[0].wait()

    def spatial_in(at):
        normed, _ = normalize(x_ref[at, :].astype(F32))
        hid0[at, :] = (normed * (1.0 + mod(scale0)) + mod(shift0)).astype(BF16)

    by_rows(spatial_in)
    loads[1].wait()

    pk0[...] = nn(hid0[...], w0[...]).astype(BF16)

    ids = jnp.broadcast_to(ids_ref[...], (rows_of, rows_of))
    mask = ids == ids.T

    def part(n, h):
        return pk0[:, (2 * n + h) * HD : (2 * n + h + 1) * HD]

    for h in range(HEADS):
        p = softmax(part(0, h), part(1, h), mask)
        probs[h] = p
        att = nn(p.astype(BF16), part(2, h)).astype(BF16)
        att0[:, h * HD : (h + 1) * HD] = att
        b0[h, 3] = att
    loads[2].wait()

    def middle(at):
        mid[:, at] = (
            x_ref[:, at].astype(F32) + mod_ref[gate0 : gate0 + 1, at] * nn(att0[...], wo0[:, at])
        ).astype(BF16)

    by_columns(middle)

    def temporal_in(at):
        normed, _ = normalize(mid[at, :].astype(F32))
        hid1[at, :] = (normed * (1.0 + mod(scale1)) + mod(shift1)).astype(BF16)

    by_rows(temporal_in)
    loads[3].wait()

    def gate_top(at):
        g1[at, :] = (mod(gate1) * cot_ref[at, :].astype(F32)).astype(BF16)

    by_rows(gate_top)
    loads[4].wait()
    d_att1 = nt(g1[...], wo1[...]).astype(BF16)
    for h in range(HEADS):
        out_s[h, 3] = d_att1[:, h * HD : (h + 1) * HD]

    pixels = rows_of // FRAMES

    def pixel_rows(n):
        return pl.ds(pl.multiple_of(n * pixels, pixels), pixels)

    mine_rows, heads, first_kinds = pixel_rows(frame), pl.ds(0, HEADS), pl.ds(0, 3)
    pl.semaphore_wait(barrier, len(peers))
    gone_d = [
        send(out_s.at[heads, 3, pixel_rows(at)], in_s.at[heads, 3, mine_rows], peer) for at, peer in clip
    ]
    loads[5].wait()
    packed = nn(hid1[...], w1[...]).astype(BF16)
    for n in range(3):
        for h in range(HEADS):
            out_s[h, n] = packed[:, (2 * n + h) * HD : (2 * n + h + 1) * HD]
    gone = [
        [
            send(out_s.at[h, first_kinds, pixel_rows(at)], in_s.at[h, first_kinds, mine_rows], peer)
            for at, peer in clip
        ]
        for h in range(HEADS)
    ]

    order = (0, 4, 1, 5, 2, 6, 3, 7, 8, 12, 9, 13, 10, 14, 11, 15, 16, 17)
    own_tokens, sib_tokens = pl.ds(0, rows_of), pl.ds(rows_of, rows_of)

    def flip(src, dst, n):
        size = 4 * BLOCK_ROWS
        for top in range(0, features, size):
            turned = src[:, top : top + size].T
            for block in range(0, size, BLOCK_ROWS):
                for at, tile in enumerate(order):
                    dst[n, top + block + at * 16 : top + block + at * 16 + 16, 0:rows_of] = turned[
                        block + tile * 16 : block + tile * 16 + 16, :
                    ]
        return send(dst.at[n, :, own_tokens], dst.at[n, :, sib_tokens], sibling)

    shared1 = [flip(hid1, left1, 0), flip(g1, left1, 1)]

    pixel_row = lax.bitwise_and(lax.broadcasted_iota(jnp.int32, (rows_of, rows_of), 0), pixels - 1)
    pixel_col = lax.bitwise_and(lax.broadcasted_iota(jnp.int32, (rows_of, rows_of), 1), pixels - 1)
    same_pixel = pixel_row == pixel_col
    came = []
    arrived(gone_d)
    for h in range(HEADS):
        in_s[h, :, mine_rows, :] = out_s[h, :, mine_rows, :]
        arrived(gone[h])
        query, key, value, d_out = [in_s[h, n] for n in range(UNITS)]
        p = softmax(query, key, same_pixel)
        out_p[h, 3] = nn(p.astype(BF16), value).astype(BF16)
        for n, part_of in enumerate(attend_back(query, key, value, p, d_out)):
            out_p[h, n] = part_of
        came.append([
            send(out_p.at[h, :, pixel_rows(at)], back.at[h, :, mine_rows], peer) for at, peer in clip
        ])
    shared0 = [flip(hid0, left0, 0)]
    for h in range(HEADS):
        back[h, :, mine_rows, :] = out_p[h, :, mine_rows, :]
        arrived(came[h])
    kinds = pl.ds(pl.multiple_of(2 * core, 2), 2)
    sib_kinds = pl.ds(pl.multiple_of(2 * (1 - core), 2), 2)
    shared1.append(send(back.at[heads, sib_kinds], sib_b1, sibling))

    def tile_for(z_at, hi_at, half_at):
        group = 2 * hi_at + half_at
        ahead = lax.max(36 * z_at + 35 - SLOT * group, 0)
        return lax.min(lax.div(ahead, 4 * SLOT), 4 - hi_at)

    z_half = lax.rem(z, 2)
    sources = [(hi_at, half_at) for hi_at in range(2) for half_at in range(2)]
    slot = lax.broadcasted_iota(jnp.int32, (2 * SLOT, 4 * SLOT), 0)
    tile_row = lax.broadcasted_iota(jnp.int32, (2 * SLOT, 4 * SLOT), 1)
    have = lax.bitwise_and(tile_row, SLOT - 1)
    for n, (hi_at, half_at) in enumerate(sources):
        top = 4 * SLOT * tile_for(z, hi_at, half_at) + SLOT * (2 * hi_at + half_at) - 36 * z
        have = jnp.where(lax.shift_right_logical(tile_row, 4) == n, have + top, have)
    within = lax.bitwise_and(slot, SLOT - 1)
    want = (2 * lax.shift_right_logical(slot, 4) + x_hi) * OWN + within
    pick = jnp.where((have == want) & (within < OWN), 1.0, 0.0).astype(BF16)

    def reduction(box, t, b):
        (_, xa, xc, xm, xb, xu, ya, yc, ym, yb, yu, x2, y2, tz, zr, zu, zx, zy, last_out, last_in,
         held, gather, merged, final) = box

        def rows(x_at, y_at, offset):
            start = (lax.rem(x_at, 2) * 4 + y_at) * BLOCK_ROWS + offset + X_ROWS * lax.div(x_at, 2)
            return pl.ds(pl.multiple_of(start, 16), X_ROWS)

        def x_src(a, b):
            return t.at[rows(a, b, 0)]

        def y_src(a, b):
            return t.at[rows(b, a, 2 * X_ROWS)]

        def total2(one, two):
            return (one.astype(F32) + two.astype(F32)).astype(BF16)

        def far_sends(me, src, into, right, left):
            far = turn(me, 2, 4)
            return (
                [send(src(far, b), into.at[b], right) for b in (0, 1)]
                + [send(src(far, b), into.at[b], left) for b in (2, 3)]
            )

        def near_sends(me, src, into, right, left):
            return (
                [send(src(turn(me, 1, 4), b), into.at[b], right) for b in (2, 3)]
                + [send(src(turn(me, 3, 4), b), into.at[b], left) for b in (0, 1)]
            )

        def relay(me, src, box_in, kept, into, far, right, left):
            outs = []
            for n in (0, 2, 1, 3):
                far[n].wait_recv()
                kept[n] = total2(box_in[n], src(turn(me, 1 if n < 2 else 3, 4), n)[...])
                outs.append(send(kept.at[n], into.at[n], right if n < 2 else left))
            return outs

        def finish(me, src, near, into, copies, result):
            arrived(copies)
            for b in range(4):
                result[b] = (
                    src(me, b)[...].astype(F32) + near[b].astype(F32) + into[b].astype(F32)
                ).astype(BF16)

        half = X_ROWS // 2

        def second_start(me, kept, into, ring):
            return [send(kept.at[turn(me, k, 4)], into.at[n], peer) for n, (k, peer) in enumerate(ring)]

        def second_finish(me, kept, into, copies, offset):
            arrived(copies)
            total = kept[me].astype(F32)
            for n in range(3):
                total = total + into[n].astype(F32)
            total = total.astype(BF16)
            for u in range(UNITS):
                for hf in range(2):
                    last_out[2 * u + hf, offset : offset + half, :] = total[
                        hf * half : (hf + 1) * half, u * HD : (u + 1) * HD
                    ]

        def start():
            x_far_sends = far_sends(x, x_src, xa, x_right, x_left)
            y_far_sends = far_sends(y, y_src, ya, y_right, y_left)
            x_near = near_sends(x, x_src, xb, x_right, x_left)
            y_near = near_sends(y, y_src, yb, y_right, y_left)
            for u in range(UNITS):
                for hf in range(2):
                    for a in range(8):
                        top = a * BLOCK_ROWS + 4 * X_ROWS + Z_ROWS * hf
                        tz[2 * u + hf, a] = t[top : top + Z_ROWS, u * HD : (u + 1) * HD]
            z_sends = [send(tz.at[turn(z, k, 8)], zr.at[k - 1], z_peers[k]) for k in z_order]
            yield
            x_relays = relay(x, x_src, xa, xm, xc, x_far_sends, x_right, x_left)
            y_relays = relay(y, y_src, ya, ym, yc, y_far_sends, y_right, y_left)
            yield
            finish(x, x_src, xb, xc, x_near + x_relays, xu)
            x_second = second_start(y, xu, x2, y_ring)
            finish(y, y_src, yb, yc, y_near + y_relays, yu)
            y_second = second_start(x, yu, y2, x_ring)
            arrived(z_sends)
            total = tz[z].astype(F32)
            for k in range(7):
                total = total + zr[k].astype(F32)
            zu[...] = total.astype(BF16)

            def quad(x_lo_at):
                return pl.ds(pl.multiple_of(x_lo_at * 4, 4), 4)

            z_first = [
                send(zu.at[quad(x_lo)], zx.at[0], x_far),
                send(zu.at[quad(1 - x_lo)], zx.at[1], x_right),
                send(zu.at[quad(1 - x_lo)], zx.at[2], x_left),
            ]
            yield
            second_finish(y, xu, x2, x_second, 0)
            second_finish(x, yu, y2, y_second, half)
            last = [send(last_out.at[turn(z, k, 8)], last_in.at[k - 1], z_peers[k]) for k in z_order]
            arrived(z_first)
            total = zu[quad(x_lo)].astype(F32)
            for n in range(3):
                total = total + zx[n].astype(F32)
            zx[3] = total.astype(BF16)
            z_second = [send(zx.at[3, turn(y, k, 4)], zy.at[n], peer) for n, (k, peer) in enumerate(y_ring)]
            yield
            arrived(last)
            total = last_out[z].astype(F32)
            for k in range(7):
                total = total + last_in[k].astype(F32)
            for k in range(4):
                held[k] = total[k * SLOT : (k + 1) * SLOT, :].astype(BF16)
            arrived(z_second)
            total = zx[3, y].astype(F32)
            for n in range(3):
                total = total + zy[n].astype(F32)
            held[4] = total.astype(BF16)
            tiles_out = {k: held.at[tile_for(turn(z, k, 8), x_hi, z_half)] for k in z_order}
            gathers = [send(tiles_out[k], gather.at[x_hi, z], z_peers[k]) for k in z_order]
            gathers += [send(tiles_out[k], gather.at[x_hi, z], far_z_peers[k]) for k in z_order]
            own_tile = held.at[tile_for(z, x_hi, z_half)]
            gathers.append(send(own_tile, gather.at[x_hi, z], x_far))
            gather[x_hi, z] = own_tile[...]
            yield
            arrived(gathers)
            tiles = jnp.concatenate(
                [
                    jnp.concatenate([gather[hi_at, 2 * u + half_at] for u in range(UNITS)], axis=1)
                    for hi_at, half_at in sources
                ],
                axis=0,
            )
            owned = nn(pick, tiles).astype(BF16)
            for n in range(2):
                merged[n] = owned[n * SLOT : (n + 1) * SLOT, :]
            swap = send(merged.at[1 - core], final, sibling)
            yield
            scale = 1.0 / math.sqrt(rows_of * lax.axis_size("seq") * lax.axis_size("rep"))
            same = merged[core].astype(F32) * scale
            arrived([swap])
            others = final[...].astype(F32) * scale
            cores = [jnp.where(core == 0, same, others), jnp.where(core == 0, others, same)]
            both = jnp.concatenate(cores, axis=1).astype(BF16)
            for i in range(OWN):
                qkv_ref[i, b : b + 1, :] = both[i : i + 1, : 6 * HD]
                att_ref[i, b : b + 1, :] = both[i : i + 1, 6 * HD :]
            yield

        return start()

    def weight_sums(t, left, own, theirs):
        for n in range(2):
            right = jnp.concatenate(
                [
                    jnp.concatenate([own[h, 2 * core + n] for h in range(HEADS)], axis=1),
                    jnp.concatenate([theirs[h, n] for h in range(HEADS)], axis=1),
                ],
                axis=0,
            )
            source = core if n == 1 else 0

            t[:, 2 * n * HD : 2 * (n + 1) * HD] = nn(left[source], right).astype(BF16)

    def input_back(src, weight):
        d_packed = jnp.concatenate([src[h, n] for n in range(3) for h in range(HEADS)], axis=1)

        def body(at):
            acc[:, at] = nt(d_packed, weight[at, :])

        by_columns(body)

    input_back(back, w1)
    t1, t0 = boxes[1][0], boxes[0][0]
    arrived(shared1)
    weight_sums(t1, left1, back, sib_b1)
    steps1 = reduction(boxes[1], t1, 1)
    next(steps1)

    d_mid_ref = hid1

    def temporal_back(at):
        normed, inv_std = normalize(mid[at, :].astype(F32))
        term = norm_back(acc[at, :] * (1.0 + mod(scale1)), normed, inv_std)
        d_mid = (cot_ref[at, :].astype(F32) + term).astype(BF16)
        d_mid_ref[at, :] = d_mid
        g0[at, :] = (mod(gate0) * d_mid.astype(F32)).astype(BF16)

    by_rows(temporal_back)

    shared0.append(flip(g0, left0, 1))
    d_att0 = nt(g0[...], wo0[...]).astype(BF16)
    for h in range(HEADS):
        grads = attend_back(part(0, h), part(1, h), part(2, h), probs[h], d_att0[:, h * HD : (h + 1) * HD])
        for n, part_of in enumerate(grads):
            b0[h, n] = part_of
    shared0.append(send(b0.at[heads, sib_kinds], sib_b0, sibling))
    input_back(b0, w0)
    next(steps1)
    arrived(shared0)
    weight_sums(t0, left0, b0, sib_b0)
    steps0 = reduction(boxes[0], t0, 0)
    next(steps0)

    def spatial_back(at):
        normed, inv_std = normalize(x_ref[at, :].astype(F32))
        term = norm_back(acc[at, :] * (1.0 + mod(scale0)), normed, inv_std)
        grad_ref[at, :] = (d_mid_ref[at, :].astype(F32) + term).astype(BF16)

    by_rows(spatial_back)
    next(steps0)
    next(steps1)
    next(steps0)
    next(steps1)
    next(steps0)
    next(steps1)
    next(steps0)
    next(steps1)
    next(steps0)
    next(steps1)
    next(steps0)
    for copy in used:
        copy.wait_send()


def whole(tokens, ids, cotangent, modulation, w_qkv, w_out):
    _, rows, features = tokens.shape
    inner = HEADS * HD

    def vmem(*shape, dtype=BF16):
        return pltpu.VMEM(shape, dtype)

    full = lambda: vmem(rows, features)
    pooled = lambda: vmem(2, features, 2 * rows)
    units = lambda: vmem(HEADS, UNITS, rows, HD)
    ring = [vmem(4, X_ROWS, WIDE) for _ in range(5)]
    second = [vmem(3, X_ROWS, WIDE)]
    reduction = (
        [vmem(features, WIDE)] + ring + ring + second + second + [
            vmem(8, 8, Z_ROWS, HD), vmem(7, 8, Z_ROWS, HD), vmem(8, Z_ROWS, HD),
            vmem(4, 4, Z_ROWS, HD), vmem(3, Z_ROWS, HD),
            vmem(8, X_ROWS, HD), vmem(7, X_ROWS, HD),
            vmem(5, SLOT, HD), vmem(2, 8, SLOT, HD), vmem(2, SLOT, WIDE), vmem(SLOT, WIDE),
        ]
    )
    scratch = [
        full(), full(), vmem(features, 3 * inner), vmem(features, 3 * inner),
        vmem(inner, features), vmem(inner, features),
        full(), full(), full(), full(), full(), vmem(rows, features, dtype=F32),
        vmem(rows, 3 * inner), vmem(HEADS, rows, rows, dtype=F32), vmem(rows, inner),
    ] + [pooled(), pooled()] + [units() for _ in range(5)] + [
        vmem(HEADS, 2, rows, HD), vmem(HEADS, 2, rows, HD),
    ] + reduction + reduction + [
        pltpu.SemaphoreType.DMA((6,)),
        pltpu.SemaphoreType.DMA((176,)),
        pltpu.SemaphoreType.DMA((176,)),
    ]
    in_vmem = pl.BlockSpec(memory_space=pltpu.VMEM)
    anywhere = pl.BlockSpec(memory_space=pl.ANY)
    return pl.pallas_call(
        whole_kernel,
        out_shape=(
            pltpu.VMEM((rows, features), BF16),
            pltpu.VMEM((OWN, 2, 3 * inner), BF16),
            pltpu.VMEM((OWN, 2, inner), BF16),
        ),
        in_specs=[anywhere, in_vmem, anywhere, in_vmem, anywhere, anywhere],
        out_specs=(in_vmem, in_vmem, in_vmem),
        scratch_shapes=scratch,
        compiler_params=pltpu.CompilerParams(
            collective_id=0, has_side_effects=True, vmem_limit_bytes=60 * 2**20
        ),
    )(tokens, ids, cotangent, modulation, w_qkv, w_out)


def local(tokens, window_ids, cotangent, modulation, w_qkv, w_out):
    d_tokens, qkv, out = whole(tokens, window_ids, cotangent, modulation, w_qkv, w_out)
    return (d_tokens[None], qkv.transpose(1, 0, 2), out.transpose(1, 2, 0))


def solution(mesh):
    in_specs = (P("rep", "seq", None), P("rep", "seq"), P("rep", "seq", None), P(), P(), P())
    out_specs = (
        P("rep", "seq", None),
        P(None, ("seq", "rep"), None),
        P(None, None, ("seq", "rep")),
    )
    return jax.shard_map(local, mesh=mesh, in_specs=in_specs, out_specs=out_specs, check_vma=False)
```

```python
import math

import jax
import jax.numpy as jnp
from jax import lax
from jax.experimental import pallas as pl
from jax.experimental.pallas import tpu as pltpu
from jax.sharding import PartitionSpec as P

MESH = pl.DeviceIdType.MESH
BF16, F32 = jnp.bfloat16, jnp.float32
HD = 128
HEADS = 2
FRAMES = 8
UNITS = 4
WIDE = UNITS * HD
BLOCK_ROWS = 288
X_ROWS, Z_ROWS = 64, 16
OWN = 9
SLOT = 16
epsilon = 1e-06
factor_of_scores = HD ** (-0.5)


def nn(left, right):
    return lax.dot_general(left, right, (((1,), (0,)), ((), ())), preferred_element_type=F32)


def nt(left, right):
    return lax.dot_general(left, right, (((1,), (1,)), ((), ())), preferred_element_type=F32)


def softmax(query, key, mask):
    scores = jnp.where(mask, nt(query, key) * factor_of_scores, -1e30)
    expd = jnp.exp(scores - jnp.max(scores, axis=-1, keepdims=True))
    return expd / jnp.sum(expd, axis=-1, keepdims=True)


def attend_back(query, key, value, probs, d_out):
    d_value = nn(probs.astype(BF16).T, d_out)
    d_prob = nt(d_out, value)
    d_score = (probs * (d_prob - jnp.sum(probs * d_prob, axis=-1, keepdims=True))).astype(BF16)
    d_query = nn(d_score, key) * factor_of_scores
    d_key = nn(d_score.T, query) * factor_of_scores
    return d_query.astype(BF16), d_key.astype(BF16), d_value.astype(BF16)


def normalize(values):
    centered = values - jnp.mean(values, axis=-1, keepdims=True)
    inv_std = lax.rsqrt(jnp.mean(centered * centered, axis=-1, keepdims=True) + epsilon)
    return centered * inv_std, inv_std


def norm_back(d_normed, normed, inv_std):
    return inv_std * (
        d_normed
        - jnp.mean(d_normed, axis=-1, keepdims=True)
        - normed * jnp.mean(d_normed * normed, axis=-1, keepdims=True)
    )


def whole_kernel(tokens_hbm, ids_ref, cot_hbm, mod_ref, qkv_hbm, out_hbm,
                 grad_ref, qkv_ref, att_ref,
                 x_ref, cot_ref, w0, w1, wo0, wo1,
                 hid0, hid1, mid, g1, g0, acc, pk0, probs, att0,
                 left0, left1, out_s, in_s, out_p, back, b0, sib_b1, sib_b0,
                 *rest):
    per_block = 24
    boxes = [rest[:per_block], rest[per_block : 2 * per_block]]
    load_sem, send_sem, recv_sem = rest[2 * per_block :]

    seq = lax.axis_index("seq")
    x_hi = lax.axis_index("rep")
    core = lax.rem(seq, 2)
    z = lax.rem(lax.div(seq, 2), 8)
    y = lax.rem(lax.div(seq, 16), 4)
    x_lo = lax.div(seq, 64)
    x = 2 * x_hi + x_lo
    frame = x_lo * 4 + y

    loads, load_count = [], 0
    for src, dst, pieces in [
        (tokens_hbm.at[0], x_ref, 1), (qkv_hbm.at[0], w0, 4), (out_hbm.at[0], wo0, 1),
        (cot_hbm.at[0], cot_ref, 1), (out_hbm.at[1], wo1, 1), (qkv_hbm.at[1], w1, 4),
    ]:
        size = dst.shape[0] // pieces
        loads.append([])
        for n in range(pieces):
            at = pl.ds(n * size, size)
            loads[-1].append(pltpu.make_async_copy(src.at[at], dst.at[at], load_sem.at[load_count]))
            load_count += 1

    def begin(*which):
        for n in which:
            for copy in loads[n]:
                copy.start()

    def loaded(n):
        for copy in loads[n]:
            copy.wait()

    begin(0, 1)

    def device(x_at, y_at, z_at, core_at):
        return {"seq": ((lax.rem(x_at, 2) * 4 + y_at) * 8 + z_at) * 2 + core_at, "rep": lax.div(x_at, 2)}

    def turn(at, step, size):
        return lax.rem(at + step, size)

    x_right, x_left = device(turn(x, 1, 4), y, z, core), device(turn(x, 3, 4), y, z, core)
    x_far_at = turn(x, 2, 4)
    z_order = (4, 3, 5, 2, 6, 1, 7)
    z_peers = {k: device(x, y, turn(z, k, 8), core) for k in z_order}
    sibling, x_far = device(x, y, z, 1 - core), device(x_far_at, y, z, core)
    far_z_peers = {k: device(x_far_at, y, turn(z, k, 8), core) for k in z_order}
    other = 2 * x_hi + 1 - x_lo
    clip = []
    for cross, step in ((1, 2), (1, 1), (1, 3), (1, 0), (0, 2), (0, 1), (0, 3)):
        y_at = turn(y, step, 4)
        frame_at = (1 - x_lo if cross else x_lo) * 4 + y_at
        clip.append((frame_at, device(other if cross else x, y_at, z, core)))
    y_far, y_right, y_left = clip[4][1], clip[5][1], clip[6][1]

    x_ring = ((2, x_far), (1, x_right), (3, x_left))
    y_ring = ((2, y_far), (1, y_right), (3, y_left))

    barrier = pltpu.get_barrier_semaphore()
    peers = [x_right, x_left, sibling, x_far] + [peer for _, peer in clip]
    peers += list(z_peers.values()) + list(far_z_peers.values())
    for peer in peers:
        pl.semaphore_signal(barrier, inc=1, device_id=peer, device_id_type=MESH)

    used = []

    def send(src, dst, peer):
        at = len(used)
        copy = pltpu.make_async_remote_copy(
            src_ref=src, dst_ref=dst, send_sem=send_sem.at[at], recv_sem=recv_sem.at[at],
            device_id=peer, device_id_type=MESH,
        )
        copy.start()
        used.append(copy)
        return copy

    def arrived(copies):
        for copy in copies:
            copy.wait_recv()

    gone_already = []

    def departed(copies):
        for copy in copies:
            copy.wait_send()
        gone_already.extend(copies)

    rows_of = x_ref.shape[0]
    features = x_ref.shape[1]
    shift0, scale0, gate0, shift1, scale1, gate1 = range(6)

    def mod(n):
        return mod_ref[n : n + 1, :]

    def by_rows(body):
        def step(i, carry):
            body(pl.ds(pl.multiple_of(i * 16, 16), 16))
            return carry

        lax.fori_loop(0, rows_of // 16, step, 0, unroll=8)

    def by_columns(body, size=1152):
        def step(i, carry):
            body(pl.ds(pl.multiple_of(i * size, size), size))
            return carry

        lax.fori_loop(0, features // size, step, 0)

    loaded(0)

    def spatial_in(at):
        normed, _ = normalize(x_ref[at, :].astype(F32))
        hid0[at, :] = (normed * (1.0 + mod(scale0)) + mod(shift0)).astype(BF16)

    by_rows(spatial_in)
    loaded(1)
    begin(2, 3, 4, 5)

    pk0[...] = nn(hid0[...], w0[...]).astype(BF16)

    ids = jnp.broadcast_to(ids_ref[...], (rows_of, rows_of))
    mask = ids == ids.T

    def part(n, h):
        return pk0[:, (2 * n + h) * HD : (2 * n + h + 1) * HD]

    for h in range(HEADS):
        p = softmax(part(0, h), part(1, h), mask)
        probs[h] = p
        att = nn(p.astype(BF16), part(2, h)).astype(BF16)
        att0[:, h * HD : (h + 1) * HD] = att
        b0[h, 3] = att
    loaded(2)

    def middle(at):
        mid[:, at] = (
            x_ref[:, at].astype(F32) + mod_ref[gate0 : gate0 + 1, at] * nn(att0[...], wo0[:, at])
        ).astype(BF16)

    by_columns(middle)

    def temporal_in(at):
        normed, _ = normalize(mid[at, :].astype(F32))
        hid1[at, :] = (normed * (1.0 + mod(scale1)) + mod(shift1)).astype(BF16)

    by_rows(temporal_in)
    loaded(3)

    def gate_top(at):
        g1[at, :] = (mod(gate1) * cot_ref[at, :].astype(F32)).astype(BF16)

    by_rows(gate_top)
    loaded(4)
    d_att1 = nt(g1[...], wo1[...]).astype(BF16)
    for h in range(HEADS):
        out_s[h, 3] = d_att1[:, h * HD : (h + 1) * HD]

    pixels = rows_of // FRAMES

    def pixel_rows(n):
        return pl.ds(pl.multiple_of(n * pixels, pixels), pixels)

    mine_rows, heads, first_kinds = pixel_rows(frame), pl.ds(0, HEADS), pl.ds(0, 3)
    pl.semaphore_wait(barrier, len(peers))
    gone_d = [
        send(out_s.at[heads, 3, pixel_rows(at)], in_s.at[heads, 3, mine_rows], peer) for at, peer in clip
    ]
    loaded(5)
    packed = nn(hid1[...], w1[...]).astype(BF16)
    for n in range(3):
        for h in range(HEADS):
            out_s[h, n] = packed[:, (2 * n + h) * HD : (2 * n + h + 1) * HD]

    def send_head(h):
        return [
            send(out_s.at[h, first_kinds, pixel_rows(at)], in_s.at[h, first_kinds, mine_rows], peer)
            for at, peer in clip
        ]

    gone = [send_head(0)]

    order = (0, 4, 1, 5, 2, 6, 3, 7, 8, 12, 9, 13, 10, 14, 11, 15, 16, 17)
    own_tokens, sib_tokens = pl.ds(0, rows_of), pl.ds(rows_of, rows_of)

    def flip(src, dst, n):
        size = 4 * BLOCK_ROWS
        for top in range(0, features, size):
            turned = src[:, top : top + size].T
            for block in range(0, size, BLOCK_ROWS):
                for at, tile in enumerate(order):
                    dst[n, top + block + at * 16 : top + block + at * 16 + 16, 0:rows_of] = turned[
                        block + tile * 16 : block + tile * 16 + 16, :
                    ]
        return send(dst.at[n, :, own_tokens], dst.at[n, :, sib_tokens], sibling)

    shared1 = [flip(hid1, left1, 0), flip(g1, left1, 1)]
    departed(gone[0])
    gone.append(send_head(1))

    pixel_row = lax.bitwise_and(lax.broadcasted_iota(jnp.int32, (rows_of, rows_of), 0), pixels - 1)
    pixel_col = lax.bitwise_and(lax.broadcasted_iota(jnp.int32, (rows_of, rows_of), 1), pixels - 1)
    same_pixel = pixel_row == pixel_col
    came = []
    arrived(gone_d)
    for h in range(HEADS):
        in_s[h, :, mine_rows, :] = out_s[h, :, mine_rows, :]
        arrived(gone[h])
        query, key, value, d_out = [in_s[h, n] for n in range(UNITS)]
        p = softmax(query, key, same_pixel)
        out_p[h, 3] = nn(p.astype(BF16), value).astype(BF16)
        for n, part_of in enumerate(attend_back(query, key, value, p, d_out)):
            out_p[h, n] = part_of
        came.append([
            send(out_p.at[h, :, pixel_rows(at)], back.at[h, :, mine_rows], peer) for at, peer in clip
        ])
    shared0 = [flip(hid0, left0, 0)]
    for h in range(HEADS):
        back[h, :, mine_rows, :] = out_p[h, :, mine_rows, :]
        arrived(came[h])
    kinds = pl.ds(pl.multiple_of(2 * core, 2), 2)
    sib_kinds = pl.ds(pl.multiple_of(2 * (1 - core), 2), 2)
    shared1.append(send(back.at[heads, sib_kinds], sib_b1, sibling))

    def tile_for(z_at, hi_at, half_at):
        group = 2 * hi_at + half_at
        ahead = lax.max(36 * z_at + 35 - SLOT * group, 0)
        return lax.min(lax.div(ahead, 4 * SLOT), 4 - hi_at)

    z_half = lax.rem(z, 2)
    sources = [(hi_at, half_at) for hi_at in range(2) for half_at in range(2)]
    slot = lax.broadcasted_iota(jnp.int32, (2 * SLOT, 4 * SLOT), 0)
    tile_row = lax.broadcasted_iota(jnp.int32, (2 * SLOT, 4 * SLOT), 1)
    have = lax.bitwise_and(tile_row, SLOT - 1)
    for n, (hi_at, half_at) in enumerate(sources):
        top = 4 * SLOT * tile_for(z, hi_at, half_at) + SLOT * (2 * hi_at + half_at) - 36 * z
        have = jnp.where(lax.shift_right_logical(tile_row, 4) == n, have + top, have)
    within = lax.bitwise_and(slot, SLOT - 1)
    want = (2 * lax.shift_right_logical(slot, 4) + x_hi) * OWN + within
    pick = jnp.where((have == want) & (within < OWN), 1.0, 0.0).astype(BF16)

    def reduction(box, t, b):
        (_, xa, xc, xm, xb, xu, ya, yc, ym, yb, yu, x2, y2, tz, zr, zu, zx, zy, last_out, last_in,
         held, gather, merged, final) = box

        def rows(x_at, y_at, offset):
            start = (lax.rem(x_at, 2) * 4 + y_at) * BLOCK_ROWS + offset + X_ROWS * lax.div(x_at, 2)
            return pl.ds(pl.multiple_of(start, 16), X_ROWS)

        def x_src(a, b):
            return t.at[rows(a, b, 0)]

        def y_src(a, b):
            return t.at[rows(b, a, 2 * X_ROWS)]

        def total2(one, two):
            return (one.astype(F32) + two.astype(F32)).astype(BF16)

        def far_sends(me, src, into, right, left):
            far = turn(me, 2, 4)
            return (
                [send(src(far, b), into.at[b], right) for b in (0, 1)]
                + [send(src(far, b), into.at[b], left) for b in (2, 3)]
            )

        def near_sends(me, src, into, right, left):
            return (
                [send(src(turn(me, 1, 4), b), into.at[b], right) for b in (2, 3)]
                + [send(src(turn(me, 3, 4), b), into.at[b], left) for b in (0, 1)]
            )

        def relay(me, src, box_in, kept, into, far, right, left):
            outs = []
            for n in (0, 2, 1, 3):
                far[n].wait_recv()
                kept[n] = total2(box_in[n], src(turn(me, 1 if n < 2 else 3, 4), n)[...])
                outs.append(send(kept.at[n], into.at[n], right if n < 2 else left))
            return outs

        def finish(me, src, near, into, copies, result):
            arrived(copies)
            for b in range(4):
                result[b] = (
                    src(me, b)[...].astype(F32) + near[b].astype(F32) + into[b].astype(F32)
                ).astype(BF16)

        half = X_ROWS // 2

        def second_start(me, kept, into, ring):
            return [send(kept.at[turn(me, k, 4)], into.at[n], peer) for n, (k, peer) in enumerate(ring)]

        def second_finish(me, kept, into, copies, offset):
            arrived(copies)
            total = kept[me].astype(F32)
            for n in range(3):
                total = total + into[n].astype(F32)
            total = total.astype(BF16)
            for u in range(UNITS):
                for hf in range(2):
                    last_out[2 * u + hf, offset : offset + half, :] = total[
                        hf * half : (hf + 1) * half, u * HD : (u + 1) * HD
                    ]

        def start():
            x_far_sends = far_sends(x, x_src, xa, x_right, x_left)
            y_far_sends = far_sends(y, y_src, ya, y_right, y_left)
            for u in range(UNITS):
                for hf in range(2):
                    for a in range(8):
                        top = a * BLOCK_ROWS + 4 * X_ROWS + Z_ROWS * hf
                        tz[2 * u + hf, a] = t[top : top + Z_ROWS, u * HD : (u + 1) * HD]
            z_sends = [send(tz.at[turn(z, k, 8)], zr.at[k - 1], z_peers[k]) for k in z_order]
            yield
            x_near = near_sends(x, x_src, xb, x_right, x_left)
            y_near = near_sends(y, y_src, yb, y_right, y_left)
            yield
            x_relays = relay(x, x_src, xa, xm, xc, x_far_sends, x_right, x_left)
            y_relays = relay(y, y_src, ya, ym, yc, y_far_sends, y_right, y_left)
            yield
            finish(x, x_src, xb, xc, x_near + x_relays, xu)
            x_second = second_start(y, xu, x2, y_ring)
            finish(y, y_src, yb, yc, y_near + y_relays, yu)
            y_second = second_start(x, yu, y2, x_ring)
            arrived(z_sends)
            total = tz[z].astype(F32)
            for k in range(7):
                total = total + zr[k].astype(F32)
            zu[...] = total.astype(BF16)

            def quad(x_lo_at):
                return pl.ds(pl.multiple_of(x_lo_at * 4, 4), 4)

            z_first = [
                send(zu.at[quad(x_lo)], zx.at[0], x_far),
                send(zu.at[quad(1 - x_lo)], zx.at[1], x_right),
                send(zu.at[quad(1 - x_lo)], zx.at[2], x_left),
            ]
            yield
            second_finish(y, xu, x2, x_second, 0)
            second_finish(x, yu, y2, y_second, half)
            last = [send(last_out.at[turn(z, k, 8)], last_in.at[k - 1], z_peers[k]) for k in z_order]
            arrived(z_first)
            total = zu[quad(x_lo)].astype(F32)
            for n in range(3):
                total = total + zx[n].astype(F32)
            zx[3] = total.astype(BF16)
            z_second = [send(zx.at[3, turn(y, k, 4)], zy.at[n], peer) for n, (k, peer) in enumerate(y_ring)]
            yield
            arrived(last)
            total = last_out[z].astype(F32)
            for k in range(7):
                total = total + last_in[k].astype(F32)
            for k in range(4):
                held[k] = total[k * SLOT : (k + 1) * SLOT, :].astype(BF16)
            arrived(z_second)
            total = zx[3, y].astype(F32)
            for n in range(3):
                total = total + zy[n].astype(F32)
            held[4] = total.astype(BF16)
            tiles_out = {k: held.at[tile_for(turn(z, k, 8), x_hi, z_half)] for k in z_order}
            gathers = [send(tiles_out[k], gather.at[x_hi, z], z_peers[k]) for k in z_order]
            gathers += [send(tiles_out[k], gather.at[x_hi, z], far_z_peers[k]) for k in z_order]
            own_tile = held.at[tile_for(z, x_hi, z_half)]
            gathers.append(send(own_tile, gather.at[x_hi, z], x_far))
            gather[x_hi, z] = own_tile[...]
            yield
            arrived(gathers)
            tiles = jnp.concatenate(
                [
                    jnp.concatenate([gather[hi_at, 2 * u + half_at] for u in range(UNITS)], axis=1)
                    for hi_at, half_at in sources
                ],
                axis=0,
            )
            owned = nn(pick, tiles).astype(BF16)
            for n in range(2):
                merged[n] = owned[n * SLOT : (n + 1) * SLOT, :]
            swap = send(merged.at[1 - core], final, sibling)
            yield
            scale = 1.0 / math.sqrt(rows_of * lax.axis_size("seq") * lax.axis_size("rep"))
            same = merged[core].astype(F32) * scale
            arrived([swap])
            others = final[...].astype(F32) * scale
            cores = [jnp.where(core == 0, same, others), jnp.where(core == 0, others, same)]
            both = jnp.concatenate(cores, axis=1).astype(BF16)
            for i in range(OWN):
                qkv_ref[i, b : b + 1, :] = both[i : i + 1, : 6 * HD]
                att_ref[i, b : b + 1, :] = both[i : i + 1, 6 * HD :]
            yield

        return start()

    def weight_sums(t, left, own, theirs):
        for n in range(2):
            right = jnp.concatenate(
                [
                    jnp.concatenate([own[h, 2 * core + n] for h in range(HEADS)], axis=1),
                    jnp.concatenate([theirs[h, n] for h in range(HEADS)], axis=1),
                ],
                axis=0,
            )
            source = core if n == 1 else 0

            t[:, 2 * n * HD : 2 * (n + 1) * HD] = nn(left[source], right).astype(BF16)

    def input_back(src, weight):
        d_packed = jnp.concatenate([src[h, n] for n in range(3) for h in range(HEADS)], axis=1)

        def body(at):
            acc[:, at] = nt(d_packed, weight[at, :])

        by_columns(body)

    t1, t0 = boxes[1][0], boxes[0][0]
    arrived(shared1)
    weight_sums(t1, left1, back, sib_b1)
    steps1 = reduction(boxes[1], t1, 1)
    next(steps1)
    input_back(back, w1)

    d_mid_ref = hid1

    def temporal_back(at):
        normed, inv_std = normalize(mid[at, :].astype(F32))
        term = norm_back(acc[at, :] * (1.0 + mod(scale1)), normed, inv_std)
        d_mid = (cot_ref[at, :].astype(F32) + term).astype(BF16)
        d_mid_ref[at, :] = d_mid
        g0[at, :] = (mod(gate0) * d_mid.astype(F32)).astype(BF16)

    by_rows(temporal_back)
    next(steps1)

    shared0.append(flip(g0, left0, 1))
    d_att0 = nt(g0[...], wo0[...]).astype(BF16)
    for h in range(HEADS):
        grads = attend_back(part(0, h), part(1, h), part(2, h), probs[h], d_att0[:, h * HD : (h + 1) * HD])
        for n, part_of in enumerate(grads):
            b0[h, n] = part_of
    shared0.append(send(b0.at[heads, sib_kinds], sib_b0, sibling))
    next(steps1)
    arrived(shared0)
    weight_sums(t0, left0, b0, sib_b0)
    steps0 = reduction(boxes[0], t0, 0)
    next(steps0)

    def spatial_back(at):
        normed, inv_std = normalize(x_ref[at, :].astype(F32))
        term = norm_back(acc[at, :] * (1.0 + mod(scale0)), normed, inv_std)
        grad_ref[at, :] = (d_mid_ref[at, :].astype(F32) + term).astype(BF16)

    input_back(b0, w0)
    next(steps0)
    by_rows(spatial_back)
    next(steps0)
    next(steps1)
    next(steps0)
    next(steps1)
    next(steps0)
    next(steps1)
    next(steps0)
    next(steps1)
    next(steps0)
    next(steps1)
    next(steps0)
    for copy in used:
        if not any(copy is other for other in gone_already):
            copy.wait_send()


def whole(tokens, ids, cotangent, modulation, w_qkv, w_out):
    _, rows, features = tokens.shape
    inner = HEADS * HD

    def vmem(*shape, dtype=BF16):
        return pltpu.VMEM(shape, dtype)

    full = lambda: vmem(rows, features)
    pooled = lambda: vmem(2, features, 2 * rows)
    units = lambda: vmem(HEADS, UNITS, rows, HD)
    ring = [vmem(4, X_ROWS, WIDE) for _ in range(5)]
    second = [vmem(3, X_ROWS, WIDE)]
    reduction = (
        [vmem(features, WIDE)] + ring + ring + second + second + [
            vmem(8, 8, Z_ROWS, HD), vmem(7, 8, Z_ROWS, HD), vmem(8, Z_ROWS, HD),
            vmem(4, 4, Z_ROWS, HD), vmem(3, Z_ROWS, HD),
            vmem(8, X_ROWS, HD), vmem(7, X_ROWS, HD),
            vmem(5, SLOT, HD), vmem(2, 8, SLOT, HD), vmem(2, SLOT, WIDE), vmem(SLOT, WIDE),
        ]
    )
    scratch = [
        full(), full(), vmem(features, 3 * inner), vmem(features, 3 * inner),
        vmem(inner, features), vmem(inner, features),
        full(), full(), full(), full(), full(), vmem(rows, features, dtype=F32),
        vmem(rows, 3 * inner), vmem(HEADS, rows, rows, dtype=F32), vmem(rows, inner),
    ] + [pooled(), pooled()] + [units() for _ in range(5)] + [
        vmem(HEADS, 2, rows, HD), vmem(HEADS, 2, rows, HD),
    ] + reduction + reduction + [
        pltpu.SemaphoreType.DMA((16,)),
        pltpu.SemaphoreType.DMA((176,)),
        pltpu.SemaphoreType.DMA((176,)),
    ]
    in_vmem = pl.BlockSpec(memory_space=pltpu.VMEM)
    anywhere = pl.BlockSpec(memory_space=pl.ANY)
    return pl.pallas_call(
        whole_kernel,
        out_shape=(
            pltpu.VMEM((rows, features), BF16),
            pltpu.VMEM((OWN, 2, 3 * inner), BF16),
            pltpu.VMEM((OWN, 2, inner), BF16),
        ),
        in_specs=[anywhere, in_vmem, anywhere, in_vmem, anywhere, anywhere],
        out_specs=(in_vmem, in_vmem, in_vmem),
        scratch_shapes=scratch,
        compiler_params=pltpu.CompilerParams(
            collective_id=0, has_side_effects=True, vmem_limit_bytes=60 * 2**20
        ),
    )(tokens, ids, cotangent, modulation, w_qkv, w_out)


def local(tokens, window_ids, cotangent, modulation, w_qkv, w_out):
    d_tokens, qkv, out = whole(tokens, window_ids, cotangent, modulation, w_qkv, w_out)
    return (d_tokens[None], qkv.transpose(1, 0, 2), out.transpose(1, 2, 0))


def solution(mesh):
    in_specs = (P("rep", "seq", None), P("rep", "seq"), P("rep", "seq", None), P(), P(), P())
    out_specs = (
        P("rep", "seq", None),
        P(None, ("seq", "rep"), None),
        P(None, None, ("seq", "rep")),
    )
    return jax.shard_map(local, mesh=mesh, in_specs=in_specs, out_specs=out_specs, check_vma=False)
```

```python
import math

import jax
import jax.numpy as jnp
from jax import lax
from jax.experimental import pallas as pl
from jax.experimental.pallas import tpu as pltpu
from jax.sharding import PartitionSpec as P

MESH = pl.DeviceIdType.MESH
BF16, F32 = jnp.bfloat16, jnp.float32
HD = 128
HEADS = 2
FRAMES = 8
UNITS = 4
WIDE = UNITS * HD
BLOCK_ROWS = 288
X_ROWS, Z_ROWS = 64, 16
OWN = 9
SLOT = 16
epsilon = 1e-06
factor_of_scores = HD ** (-0.5)


def nn(left, right):
    return lax.dot_general(left, right, (((1,), (0,)), ((), ())), preferred_element_type=F32)


def nt(left, right):
    return lax.dot_general(left, right, (((1,), (1,)), ((), ())), preferred_element_type=F32)


def softmax(query, key, mask):
    scores = jnp.where(mask, nt(query, key) * factor_of_scores, -1e30)
    expd = jnp.exp(scores - jnp.max(scores, axis=-1, keepdims=True))
    return expd / jnp.sum(expd, axis=-1, keepdims=True)


def attend_back(query, key, value, probs, d_out):
    d_value = nn(probs.astype(BF16).T, d_out)
    d_prob = nt(d_out, value)
    d_score = (probs * (d_prob - jnp.sum(probs * d_prob, axis=-1, keepdims=True))).astype(BF16)
    d_query = nn(d_score, key) * factor_of_scores
    d_key = nn(d_score.T, query) * factor_of_scores
    return d_query.astype(BF16), d_key.astype(BF16), d_value.astype(BF16)


def normalize(values):
    centered = values - jnp.mean(values, axis=-1, keepdims=True)
    inv_std = lax.rsqrt(jnp.mean(centered * centered, axis=-1, keepdims=True) + epsilon)
    return centered * inv_std, inv_std


def norm_back(d_normed, normed, inv_std):
    return inv_std * (
        d_normed
        - jnp.mean(d_normed, axis=-1, keepdims=True)
        - normed * jnp.mean(d_normed * normed, axis=-1, keepdims=True)
    )


def whole_kernel(tokens_hbm, ids_hbm, cot_hbm, mod_hbm, qkv_hbm, out_hbm,
                 grad_ref, qkv_ref, att_ref,
                 x_ref, cot_ref, w0, w1, wo0, wo1,
                 hid0, hid1, mid, g1, g0, acc, pk0, probs, att0,
                 ids_ref, mod_ref, left0, left1, out_s, in_s, out_p, back, b0, sib_b1, sib_b0,
                 *rest):
    per_block = 24
    boxes = [rest[:per_block], rest[per_block : 2 * per_block]]
    load_sem, send_sem, recv_sem = rest[2 * per_block :]

    seq = lax.axis_index("seq")
    x_hi = lax.axis_index("rep")
    core = lax.rem(seq, 2)
    z = lax.rem(lax.div(seq, 2), 8)
    y = lax.rem(lax.div(seq, 16), 4)
    x_lo = lax.div(seq, 64)
    x = 2 * x_hi + x_lo
    frame = x_lo * 4 + y

    loads, load_count = [], 0
    for src, dst, pieces in [
        (tokens_hbm.at[0], x_ref, 4), (qkv_hbm.at[0], w0, 4), (out_hbm.at[0], wo0, 1),
        (cot_hbm.at[0], cot_ref, 1), (out_hbm.at[1], wo1, 1), (qkv_hbm.at[1], w1, 4),
        (mod_hbm, mod_ref, 1), (ids_hbm, ids_ref, 1),
    ]:
        size = dst.shape[0] // pieces
        loads.append([])
        for n in range(pieces):
            at = pl.ds(n * size, size)
            loads[-1].append(pltpu.make_async_copy(src.at[at], dst.at[at], load_sem.at[load_count]))
            load_count += 1

    def begin(*which):
        for n in which:
            for copy in loads[n]:
                copy.start()

    def loaded(n):
        for copy in loads[n]:
            copy.wait()

    begin(0, 6, 1, 7)

    def device(x_at, y_at, z_at, core_at):
        return {"seq": ((lax.rem(x_at, 2) * 4 + y_at) * 8 + z_at) * 2 + core_at, "rep": lax.div(x_at, 2)}

    def turn(at, step, size):
        return lax.rem(at + step, size)

    x_right, x_left = device(turn(x, 1, 4), y, z, core), device(turn(x, 3, 4), y, z, core)
    x_far_at = turn(x, 2, 4)
    z_order = (4, 3, 5, 2, 6, 1, 7)
    z_peers = {k: device(x, y, turn(z, k, 8), core) for k in z_order}
    sibling, x_far = device(x, y, z, 1 - core), device(x_far_at, y, z, core)
    far_z_peers = {k: device(x_far_at, y, turn(z, k, 8), core) for k in z_order}
    other = 2 * x_hi + 1 - x_lo
    clip = []
    for cross, step in ((1, 2), (1, 1), (1, 3), (1, 0), (0, 2), (0, 1), (0, 3)):
        y_at = turn(y, step, 4)
        frame_at = (1 - x_lo if cross else x_lo) * 4 + y_at
        clip.append((frame_at, device(other if cross else x, y_at, z, core)))
    y_far, y_right, y_left = clip[4][1], clip[5][1], clip[6][1]

    x_ring = ((2, x_far), (1, x_right), (3, x_left))
    y_ring = ((2, y_far), (1, y_right), (3, y_left))

    barrier = pltpu.get_barrier_semaphore()
    peers = [x_right, x_left, sibling, x_far] + [peer for _, peer in clip]
    peers += list(z_peers.values()) + list(far_z_peers.values())
    for peer in peers:
        pl.semaphore_signal(barrier, inc=1, device_id=peer, device_id_type=MESH)

    used = []

    def send(src, dst, peer):
        at = len(used)
        copy = pltpu.make_async_remote_copy(
            src_ref=src, dst_ref=dst, send_sem=send_sem.at[at], recv_sem=recv_sem.at[at],
            device_id=peer, device_id_type=MESH,
        )
        copy.start()
        used.append(copy)
        return copy

    def arrived(copies):
        for copy in copies:
            copy.wait_recv()

    gone_already = []

    def departed(copies):
        for copy in copies:
            copy.wait_send()
        gone_already.extend(copies)

    rows_of = x_ref.shape[0]
    features = x_ref.shape[1]
    shift0, scale0, gate0, shift1, scale1, gate1 = range(6)

    def mod(n):
        return mod_ref[n : n + 1, :]

    def by_rows(body):
        def step(i, carry):
            body(pl.ds(pl.multiple_of(i * 16, 16), 16))
            return carry

        lax.fori_loop(0, rows_of // 16, step, 0, unroll=8)

    def by_columns(body, size=1152):
        def step(i, carry):
            body(pl.ds(pl.multiple_of(i * size, size), size))
            return carry

        lax.fori_loop(0, features // size, step, 0)

    loaded(6)
    loaded(0)

    def spatial_in(at):
        normed, _ = normalize(x_ref[at, :].astype(F32))
        hid0[at, :] = (normed * (1.0 + mod(scale0)) + mod(shift0)).astype(BF16)

    by_rows(spatial_in)
    loaded(1)
    begin(2, 3, 4, 5)

    pk0[...] = nn(hid0[...], w0[...]).astype(BF16)

    loaded(7)
    ids = jnp.broadcast_to(ids_ref[...], (rows_of, rows_of))
    mask = ids == ids.T

    def part(n, h):
        return pk0[:, (2 * n + h) * HD : (2 * n + h + 1) * HD]

    for h in range(HEADS):
        p = softmax(part(0, h), part(1, h), mask)
        probs[h] = p
        att = nn(p.astype(BF16), part(2, h)).astype(BF16)
        att0[:, h * HD : (h + 1) * HD] = att
        b0[h, 3] = att
    loaded(2)

    def middle(at):
        mid[:, at] = (
            x_ref[:, at].astype(F32) + mod_ref[gate0 : gate0 + 1, at] * nn(att0[...], wo0[:, at])
        ).astype(BF16)

    by_columns(middle)

    def temporal_in(at):
        normed, _ = normalize(mid[at, :].astype(F32))
        hid1[at, :] = (normed * (1.0 + mod(scale1)) + mod(shift1)).astype(BF16)

    by_rows(temporal_in)
    loaded(3)

    def gate_top(at):
        g1[at, :] = (mod(gate1) * cot_ref[at, :].astype(F32)).astype(BF16)

    by_rows(gate_top)
    loaded(4)
    d_att1 = nt(g1[...], wo1[...]).astype(BF16)
    for h in range(HEADS):
        out_s[h, 3] = d_att1[:, h * HD : (h + 1) * HD]

    pixels = rows_of // FRAMES

    def pixel_rows(n):
        return pl.ds(pl.multiple_of(n * pixels, pixels), pixels)

    mine_rows, heads, first_kinds = pixel_rows(frame), pl.ds(0, HEADS), pl.ds(0, 3)
    pl.semaphore_wait(barrier, len(peers))
    gone_d = [
        send(out_s.at[heads, 3, pixel_rows(at)], in_s.at[heads, 3, mine_rows], peer) for at, peer in clip
    ]
    loaded(5)
    packed = nn(hid1[...], w1[...]).astype(BF16)
    for n in range(3):
        for h in range(HEADS):
            out_s[h, n] = packed[:, (2 * n + h) * HD : (2 * n + h + 1) * HD]

    def send_head(h):
        return [
            send(out_s.at[h, first_kinds, pixel_rows(at)], in_s.at[h, first_kinds, mine_rows], peer)
            for at, peer in clip
        ]

    gone = [send_head(0)]

    order = (0, 4, 1, 5, 2, 6, 3, 7, 8, 12, 9, 13, 10, 14, 11, 15, 16, 17)
    own_tokens, sib_tokens = pl.ds(0, rows_of), pl.ds(rows_of, rows_of)

    def flip(src, dst, n):
        size = 4 * BLOCK_ROWS
        for top in range(0, features, size):
            turned = src[:, top : top + size].T
            for block in range(0, size, BLOCK_ROWS):
                for at, tile in enumerate(order):
                    dst[n, top + block + at * 16 : top + block + at * 16 + 16, 0:rows_of] = turned[
                        block + tile * 16 : block + tile * 16 + 16, :
                    ]
        return send(dst.at[n, :, own_tokens], dst.at[n, :, sib_tokens], sibling)

    shared1 = [flip(hid1, left1, 0), flip(g1, left1, 1)]
    departed(gone[0])
    gone.append(send_head(1))

    pixel_row = lax.bitwise_and(lax.broadcasted_iota(jnp.int32, (rows_of, rows_of), 0), pixels - 1)
    pixel_col = lax.bitwise_and(lax.broadcasted_iota(jnp.int32, (rows_of, rows_of), 1), pixels - 1)
    same_pixel = pixel_row == pixel_col
    came = []
    arrived(gone_d)
    for h in range(HEADS):
        in_s[h, :, mine_rows, :] = out_s[h, :, mine_rows, :]
        arrived(gone[h])
        query, key, value, d_out = [in_s[h, n] for n in range(UNITS)]
        p = softmax(query, key, same_pixel)
        out_p[h, 3] = nn(p.astype(BF16), value).astype(BF16)
        for n, part_of in enumerate(attend_back(query, key, value, p, d_out)):
            out_p[h, n] = part_of
        came.append([
            send(out_p.at[h, :, pixel_rows(at)], back.at[h, :, mine_rows], peer) for at, peer in clip
        ])
    shared0 = [flip(hid0, left0, 0)]
    for h in range(HEADS):
        back[h, :, mine_rows, :] = out_p[h, :, mine_rows, :]
        arrived(came[h])
    kinds = pl.ds(pl.multiple_of(2 * core, 2), 2)
    sib_kinds = pl.ds(pl.multiple_of(2 * (1 - core), 2), 2)
    shared1.append(send(back.at[heads, sib_kinds], sib_b1, sibling))

    def tile_for(z_at, hi_at, half_at):
        group = 2 * hi_at + half_at
        ahead = lax.max(36 * z_at + 35 - SLOT * group, 0)
        return lax.min(lax.div(ahead, 4 * SLOT), 4 - hi_at)

    z_half = lax.rem(z, 2)
    sources = [(hi_at, half_at) for hi_at in range(2) for half_at in range(2)]
    slot = lax.broadcasted_iota(jnp.int32, (2 * SLOT, 4 * SLOT), 0)
    tile_row = lax.broadcasted_iota(jnp.int32, (2 * SLOT, 4 * SLOT), 1)
    have = lax.bitwise_and(tile_row, SLOT - 1)
    for n, (hi_at, half_at) in enumerate(sources):
        top = 4 * SLOT * tile_for(z, hi_at, half_at) + SLOT * (2 * hi_at + half_at) - 36 * z
        have = jnp.where(lax.shift_right_logical(tile_row, 4) == n, have + top, have)
    within = lax.bitwise_and(slot, SLOT - 1)
    want = (2 * lax.shift_right_logical(slot, 4) + x_hi) * OWN + within
    pick = jnp.where((have == want) & (within < OWN), 1.0, 0.0).astype(BF16)

    def reduction(box, t, b):
        (_, xa, xc, xm, xb, xu, ya, yc, ym, yb, yu, x2, y2, tz, zr, zu, zx, zy, last_out, last_in,
         held, gather, merged, final) = box

        def rows(x_at, y_at, offset):
            start = (lax.rem(x_at, 2) * 4 + y_at) * BLOCK_ROWS + offset + X_ROWS * lax.div(x_at, 2)
            return pl.ds(pl.multiple_of(start, 16), X_ROWS)

        def x_src(a, b):
            return t.at[rows(a, b, 0)]

        def y_src(a, b):
            return t.at[rows(b, a, 2 * X_ROWS)]

        def total2(one, two):
            return (one.astype(F32) + two.astype(F32)).astype(BF16)

        def far_sends(me, src, into, right, left):
            far = turn(me, 2, 4)
            return (
                [send(src(far, b), into.at[b], right) for b in (0, 1)]
                + [send(src(far, b), into.at[b], left) for b in (2, 3)]
            )

        def near_sends(me, src, into, right, left):
            return (
                [send(src(turn(me, 1, 4), b), into.at[b], right) for b in (2, 3)]
                + [send(src(turn(me, 3, 4), b), into.at[b], left) for b in (0, 1)]
            )

        def relay(me, src, box_in, kept, into, far, right, left):
            outs = []
            for n in (0, 2, 1, 3):
                far[n].wait_recv()
                kept[n] = total2(box_in[n], src(turn(me, 1 if n < 2 else 3, 4), n)[...])
                outs.append(send(kept.at[n], into.at[n], right if n < 2 else left))
            return outs

        def finish(me, src, near, into, copies, result):
            arrived(copies)
            for b in range(4):
                result[b] = (
                    src(me, b)[...].astype(F32) + near[b].astype(F32) + into[b].astype(F32)
                ).astype(BF16)

        half = X_ROWS // 2

        def second_start(me, kept, into, ring):
            return [send(kept.at[turn(me, k, 4)], into.at[n], peer) for n, (k, peer) in enumerate(ring)]

        def second_finish(me, kept, into, copies, offset):
            arrived(copies)
            total = kept[me].astype(F32)
            for n in range(3):
                total = total + into[n].astype(F32)
            total = total.astype(BF16)
            for u in range(UNITS):
                for hf in range(2):
                    last_out[2 * u + hf, offset : offset + half, :] = total[
                        hf * half : (hf + 1) * half, u * HD : (u + 1) * HD
                    ]

        def start():
            x_far_sends = far_sends(x, x_src, xa, x_right, x_left)
            y_far_sends = far_sends(y, y_src, ya, y_right, y_left)
            for u in range(UNITS):
                for hf in range(2):
                    for a in range(8):
                        top = a * BLOCK_ROWS + 4 * X_ROWS + Z_ROWS * hf
                        tz[2 * u + hf, a] = t[top : top + Z_ROWS, u * HD : (u + 1) * HD]
            z_sends = [send(tz.at[turn(z, k, 8)], zr.at[k - 1], z_peers[k]) for k in z_order]
            yield
            x_near = near_sends(x, x_src, xb, x_right, x_left)
            y_near = near_sends(y, y_src, yb, y_right, y_left)
            yield
            x_relays = relay(x, x_src, xa, xm, xc, x_far_sends, x_right, x_left)
            y_relays = relay(y, y_src, ya, ym, yc, y_far_sends, y_right, y_left)
            yield
            finish(x, x_src, xb, xc, x_near + x_relays, xu)
            x_second = second_start(y, xu, x2, y_ring)
            finish(y, y_src, yb, yc, y_near + y_relays, yu)
            y_second = second_start(x, yu, y2, x_ring)
            arrived(z_sends)
            total = tz[z].astype(F32)
            for k in range(7):
                total = total + zr[k].astype(F32)
            zu[...] = total.astype(BF16)

            def quad(x_lo_at):
                return pl.ds(pl.multiple_of(x_lo_at * 4, 4), 4)

            z_first = [
                send(zu.at[quad(x_lo)], zx.at[0], x_far),
                send(zu.at[quad(1 - x_lo)], zx.at[1], x_right),
                send(zu.at[quad(1 - x_lo)], zx.at[2], x_left),
            ]
            yield
            second_finish(y, xu, x2, x_second, 0)
            second_finish(x, yu, y2, y_second, half)
            last = [send(last_out.at[turn(z, k, 8)], last_in.at[k - 1], z_peers[k]) for k in z_order]
            arrived(z_first)
            total = zu[quad(x_lo)].astype(F32)
            for n in range(3):
                total = total + zx[n].astype(F32)
            zx[3] = total.astype(BF16)
            z_second = [send(zx.at[3, turn(y, k, 4)], zy.at[n], peer) for n, (k, peer) in enumerate(y_ring)]
            yield
            arrived(last)
            total = last_out[z].astype(F32)
            for k in range(7):
                total = total + last_in[k].astype(F32)
            for k in range(4):
                held[k] = total[k * SLOT : (k + 1) * SLOT, :].astype(BF16)
            arrived(z_second)
            total = zx[3, y].astype(F32)
            for n in range(3):
                total = total + zy[n].astype(F32)
            held[4] = total.astype(BF16)
            tiles_out = {k: held.at[tile_for(turn(z, k, 8), x_hi, z_half)] for k in z_order}
            gathers = [send(tiles_out[k], gather.at[x_hi, z], z_peers[k]) for k in z_order]
            gathers += [send(tiles_out[k], gather.at[x_hi, z], far_z_peers[k]) for k in z_order]
            own_tile = held.at[tile_for(z, x_hi, z_half)]
            gathers.append(send(own_tile, gather.at[x_hi, z], x_far))
            gather[x_hi, z] = own_tile[...]
            yield
            arrived(gathers)
            tiles = jnp.concatenate(
                [
                    jnp.concatenate([gather[hi_at, 2 * u + half_at] for u in range(UNITS)], axis=1)
                    for hi_at, half_at in sources
                ],
                axis=0,
            )
            owned = nn(pick, tiles).astype(BF16)
            for n in range(2):
                merged[n] = owned[n * SLOT : (n + 1) * SLOT, :]
            swap = send(merged.at[1 - core], final, sibling)
            yield
            scale = 1.0 / math.sqrt(rows_of * lax.axis_size("seq") * lax.axis_size("rep"))
            same = merged[core].astype(F32) * scale
            arrived([swap])
            others = final[...].astype(F32) * scale
            cores = [jnp.where(core == 0, same, others), jnp.where(core == 0, others, same)]
            both = jnp.concatenate(cores, axis=1).astype(BF16)
            for i in range(OWN):
                qkv_ref[i, b : b + 1, :] = both[i : i + 1, : 6 * HD]
                att_ref[i, b : b + 1, :] = both[i : i + 1, 6 * HD :]
            yield

        return start()

    def weight_sums(t, left, own, theirs):
        for n in range(2):
            right = jnp.concatenate(
                [
                    jnp.concatenate([own[h, 2 * core + n] for h in range(HEADS)], axis=1),
                    jnp.concatenate([theirs[h, n] for h in range(HEADS)], axis=1),
                ],
                axis=0,
            )
            source = core if n == 1 else 0

            t[:, 2 * n * HD : 2 * (n + 1) * HD] = nn(left[source], right).astype(BF16)

    def input_back(src, weight):
        d_packed = jnp.concatenate([src[h, n] for n in range(3) for h in range(HEADS)], axis=1)

        def body(at):
            acc[:, at] = nt(d_packed, weight[at, :])

        by_columns(body)

    t1, t0 = boxes[1][0], boxes[0][0]
    arrived(shared1)
    weight_sums(t1, left1, back, sib_b1)
    steps1 = reduction(boxes[1], t1, 1)
    next(steps1)
    input_back(back, w1)

    d_mid_ref = hid1

    def temporal_back(at):
        normed, inv_std = normalize(mid[at, :].astype(F32))
        term = norm_back(acc[at, :] * (1.0 + mod(scale1)), normed, inv_std)
        d_mid = (cot_ref[at, :].astype(F32) + term).astype(BF16)
        d_mid_ref[at, :] = d_mid
        g0[at, :] = (mod(gate0) * d_mid.astype(F32)).astype(BF16)

    by_rows(temporal_back)
    next(steps1)

    shared0.append(flip(g0, left0, 1))
    d_att0 = nt(g0[...], wo0[...]).astype(BF16)
    for h in range(HEADS):
        grads = attend_back(part(0, h), part(1, h), part(2, h), probs[h], d_att0[:, h * HD : (h + 1) * HD])
        for n, part_of in enumerate(grads):
            b0[h, n] = part_of
    shared0.append(send(b0.at[heads, sib_kinds], sib_b0, sibling))
    next(steps1)
    arrived(shared0)
    weight_sums(t0, left0, b0, sib_b0)
    steps0 = reduction(boxes[0], t0, 0)
    next(steps0)

    def spatial_back(at):
        normed, inv_std = normalize(x_ref[at, :].astype(F32))
        term = norm_back(acc[at, :] * (1.0 + mod(scale0)), normed, inv_std)
        grad_ref[at, :] = (d_mid_ref[at, :].astype(F32) + term).astype(BF16)

    input_back(b0, w0)
    next(steps0)
    by_rows(spatial_back)
    next(steps0)
    next(steps1)
    next(steps0)
    next(steps1)
    next(steps0)
    next(steps1)
    next(steps0)
    next(steps1)
    next(steps0)
    next(steps1)
    next(steps0)
    for copy in used:
        if not any(copy is other for other in gone_already):
            copy.wait_send()


def whole(tokens, ids, cotangent, modulation, w_qkv, w_out):
    _, rows, features = tokens.shape
    inner = HEADS * HD

    def vmem(*shape, dtype=BF16):
        return pltpu.VMEM(shape, dtype)

    full = lambda: vmem(rows, features)
    pooled = lambda: vmem(2, features, 2 * rows)
    units = lambda: vmem(HEADS, UNITS, rows, HD)
    ring = [vmem(4, X_ROWS, WIDE) for _ in range(5)]
    second = [vmem(3, X_ROWS, WIDE)]
    reduction = (
        [vmem(features, WIDE)] + ring + ring + second + second + [
            vmem(8, 8, Z_ROWS, HD), vmem(7, 8, Z_ROWS, HD), vmem(8, Z_ROWS, HD),
            vmem(4, 4, Z_ROWS, HD), vmem(3, Z_ROWS, HD),
            vmem(8, X_ROWS, HD), vmem(7, X_ROWS, HD),
            vmem(5, SLOT, HD), vmem(2, 8, SLOT, HD), vmem(2, SLOT, WIDE), vmem(SLOT, WIDE),
        ]
    )
    scratch = [
        full(), full(), vmem(features, 3 * inner), vmem(features, 3 * inner),
        vmem(inner, features), vmem(inner, features),
        full(), full(), full(), full(), full(), vmem(rows, features, dtype=F32),
        vmem(rows, 3 * inner), vmem(HEADS, rows, rows, dtype=F32), vmem(rows, inner),
    ] + [vmem(1, rows, dtype=jnp.int32), vmem(6, features, dtype=F32), pooled(), pooled()] + [units() for _ in range(5)] + [
        vmem(HEADS, 2, rows, HD), vmem(HEADS, 2, rows, HD),
    ] + reduction + reduction + [
        pltpu.SemaphoreType.DMA((20,)),
        pltpu.SemaphoreType.DMA((176,)),
        pltpu.SemaphoreType.DMA((176,)),
    ]
    in_vmem = pl.BlockSpec(memory_space=pltpu.VMEM)
    anywhere = pl.BlockSpec(memory_space=pl.ANY)
    return pl.pallas_call(
        whole_kernel,
        out_shape=(
            pltpu.VMEM((rows, features), BF16),
            pltpu.VMEM((OWN, 2, 3 * inner), BF16),
            pltpu.VMEM((OWN, 2, inner), BF16),
        ),
        in_specs=[anywhere] * 6,
        out_specs=(in_vmem, in_vmem, in_vmem),
        scratch_shapes=scratch,
        compiler_params=pltpu.CompilerParams(
            collective_id=0, has_side_effects=True, vmem_limit_bytes=60 * 2**20
        ),
    )(tokens, ids, cotangent, modulation, w_qkv, w_out)


def local(tokens, window_ids, cotangent, modulation, w_qkv, w_out):
    d_tokens, qkv, out = whole(tokens, window_ids, cotangent, modulation, w_qkv, w_out)
    return (d_tokens[None], qkv.transpose(1, 0, 2), out.transpose(1, 2, 0))


def solution(mesh):
    in_specs = (P("rep", "seq", None), P("rep", "seq"), P("rep", "seq", None), P(), P(), P())
    out_specs = (
        P("rep", "seq", None),
        P(None, ("seq", "rep"), None),
        P(None, None, ("seq", "rep")),
    )
    return jax.shard_map(local, mesh=mesh, in_specs=in_specs, out_specs=out_specs, check_vma=False)
```

```python
import math

import jax
import jax.numpy as jnp
from jax import lax
from jax.experimental import pallas as pl
from jax.experimental.pallas import tpu as pltpu
from jax.sharding import PartitionSpec as P

MESH = pl.DeviceIdType.MESH
BF16, F32 = jnp.bfloat16, jnp.float32
HD = 128
HEADS = 2
FRAMES = 8
UNITS = 4
WIDE = UNITS * HD
BLOCK_ROWS = 288
X_ROWS, Z_ROWS = 64, 16
OWN = 9
SLOT = 16
epsilon = 1e-06
factor_of_scores = HD ** (-0.5)


def nn(left, right):
    return lax.dot_general(left, right, (((1,), (0,)), ((), ())), preferred_element_type=F32)


def nt(left, right):
    return lax.dot_general(left, right, (((1,), (1,)), ((), ())), preferred_element_type=F32)


def softmax(query, key, mask):
    scores = jnp.where(mask, nt(query, key) * factor_of_scores, -1e30)
    expd = jnp.exp(scores - jnp.max(scores, axis=-1, keepdims=True))
    return expd / jnp.sum(expd, axis=-1, keepdims=True)


def attend_back(query, key, value, probs, d_out):
    d_value = nn(probs.astype(BF16).T, d_out)
    d_prob = nt(d_out, value)
    d_score = (probs * (d_prob - jnp.sum(probs * d_prob, axis=-1, keepdims=True))).astype(BF16)
    d_query = nn(d_score, key) * factor_of_scores
    d_key = nn(d_score.T, query) * factor_of_scores
    return d_query.astype(BF16), d_key.astype(BF16), d_value.astype(BF16)


def normalize(values):
    centered = values - jnp.mean(values, axis=-1, keepdims=True)
    inv_std = lax.rsqrt(jnp.mean(centered * centered, axis=-1, keepdims=True) + epsilon)
    return centered * inv_std, inv_std


def norm_back(d_normed, normed, inv_std):
    return inv_std * (
        d_normed
        - jnp.mean(d_normed, axis=-1, keepdims=True)
        - normed * jnp.mean(d_normed * normed, axis=-1, keepdims=True)
    )


def whole_kernel(tokens_hbm, ids_hbm, cot_hbm, mod_hbm, qkv_hbm, out_hbm,
                 grad_ref, qkv_ref, att_ref,
                 x_ref, cot_ref, w0, w1, wo0, wo1,
                 hid0, hid1, mid, g1, g0, acc, pk0, probs, att0,
                 ids_ref, mod_ref, left0, left1, out_s, in_s, out_p, back, b0, sib_b1, sib_b0,
                 *rest):
    per_block = 24
    boxes = [rest[:per_block], rest[per_block : 2 * per_block]]
    load_sem, send_sem, recv_sem = rest[2 * per_block :]

    seq = lax.axis_index("seq")
    x_hi = lax.axis_index("rep")
    core = lax.rem(seq, 2)
    z = lax.rem(lax.div(seq, 2), 8)
    y = lax.rem(lax.div(seq, 16), 4)
    x_lo = lax.div(seq, 64)
    x = 2 * x_hi + x_lo
    frame = x_lo * 4 + y

    loads, load_count = [], 0
    for src, dst, pieces in [
        (tokens_hbm.at[0], x_ref, 4), (qkv_hbm.at[0], w0, 4), (out_hbm.at[0], wo0, 1),
        (cot_hbm.at[0], cot_ref, 1), (out_hbm.at[1], wo1, 1), (qkv_hbm.at[1], w1, 4),
        (mod_hbm, mod_ref, 1), (ids_hbm, ids_ref, 1),
    ]:
        size = dst.shape[0] // pieces
        loads.append([])
        for n in range(pieces):
            at = pl.ds(n * size, size)
            loads[-1].append(pltpu.make_async_copy(src.at[at], dst.at[at], load_sem.at[load_count]))
            load_count += 1

    def begin(*which):
        for n in which:
            for copy in loads[n]:
                copy.start()

    def loaded(n):
        for copy in loads[n]:
            copy.wait()

    begin(0, 6, 1, 7)

    def device(x_at, y_at, z_at, core_at):
        return {"seq": ((lax.rem(x_at, 2) * 4 + y_at) * 8 + z_at) * 2 + core_at, "rep": lax.div(x_at, 2)}

    def turn(at, step, size):
        return lax.rem(at + step, size)

    x_right, x_left = device(turn(x, 1, 4), y, z, core), device(turn(x, 3, 4), y, z, core)
    x_far_at = turn(x, 2, 4)
    z_order = (4, 3, 5, 2, 6, 1, 7)
    z_peers = {k: device(x, y, turn(z, k, 8), core) for k in z_order}
    sibling, x_far = device(x, y, z, 1 - core), device(x_far_at, y, z, core)
    far_z_peers = {k: device(x_far_at, y, turn(z, k, 8), core) for k in z_order}
    other = 2 * x_hi + 1 - x_lo
    clip = []
    for cross, step in ((1, 2), (1, 1), (1, 3), (1, 0), (0, 2), (0, 1), (0, 3)):
        y_at = turn(y, step, 4)
        frame_at = (1 - x_lo if cross else x_lo) * 4 + y_at
        clip.append((frame_at, device(other if cross else x, y_at, z, core)))
    y_far, y_right, y_left = clip[4][1], clip[5][1], clip[6][1]

    x_ring = ((2, x_far), (1, x_right), (3, x_left))
    y_ring = ((2, y_far), (1, y_right), (3, y_left))

    barrier = pltpu.get_barrier_semaphore()
    peers = [x_right, x_left, sibling, x_far] + [peer for _, peer in clip]
    peers += list(z_peers.values()) + list(far_z_peers.values())
    for peer in peers:
        pl.semaphore_signal(barrier, inc=1, device_id=peer, device_id_type=MESH)

    used = []

    def send(src, dst, peer):
        at = len(used)
        copy = pltpu.make_async_remote_copy(
            src_ref=src, dst_ref=dst, send_sem=send_sem.at[at], recv_sem=recv_sem.at[at],
            device_id=peer, device_id_type=MESH,
        )
        copy.start()
        used.append(copy)
        return copy

    def arrived(copies):
        for copy in copies:
            copy.wait_recv()

    gone_already = []

    def departed(copies):
        for copy in copies:
            copy.wait_send()
        gone_already.extend(copies)

    rows_of = x_ref.shape[0]
    features = x_ref.shape[1]
    shift0, scale0, gate0, shift1, scale1, gate1 = range(6)

    def mod(n):
        return mod_ref[n : n + 1, :]

    def by_rows(body):
        def step(i, carry):
            body(pl.ds(pl.multiple_of(i * 16, 16), 16))
            return carry

        lax.fori_loop(0, rows_of // 16, step, 0, unroll=16)

    def by_columns(body, size=2304):
        def step(i, carry):
            body(pl.ds(pl.multiple_of(i * size, size), size))
            return carry

        lax.fori_loop(0, features // size, step, 0)

    loaded(6)
    loaded(0)

    def spatial_in(at):
        normed, _ = normalize(x_ref[at, :].astype(F32))
        hid0[at, :] = (normed * (1.0 + mod(scale0)) + mod(shift0)).astype(BF16)

    by_rows(spatial_in)
    loaded(1)
    begin(2, 3, 4, 5)

    pk0[...] = nn(hid0[...], w0[...]).astype(BF16)

    loaded(7)
    ids = jnp.broadcast_to(ids_ref[...], (rows_of, rows_of))
    mask = ids == ids.T

    def part(n, h):
        return pk0[:, (2 * n + h) * HD : (2 * n + h + 1) * HD]

    for h in range(HEADS):
        p = softmax(part(0, h), part(1, h), mask)
        probs[h] = p
        att = nn(p.astype(BF16), part(2, h)).astype(BF16)
        att0[:, h * HD : (h + 1) * HD] = att
        b0[h, 3] = att
    loaded(2)

    def middle(at):
        mid[:, at] = (
            x_ref[:, at].astype(F32) + mod_ref[gate0 : gate0 + 1, at] * nn(att0[...], wo0[:, at])
        ).astype(BF16)

    by_columns(middle)

    def temporal_in(at):
        normed, _ = normalize(mid[at, :].astype(F32))
        hid1[at, :] = (normed * (1.0 + mod(scale1)) + mod(shift1)).astype(BF16)

    by_rows(temporal_in)
    loaded(3)

    def gate_top(at):
        g1[at, :] = (mod(gate1) * cot_ref[at, :].astype(F32)).astype(BF16)

    by_rows(gate_top)
    loaded(4)
    d_att1 = nt(g1[...], wo1[...]).astype(BF16)
    for h in range(HEADS):
        out_s[h, 3] = d_att1[:, h * HD : (h + 1) * HD]

    pixels = rows_of // FRAMES

    def pixel_rows(n):
        return pl.ds(pl.multiple_of(n * pixels, pixels), pixels)

    mine_rows, heads, first_kinds = pixel_rows(frame), pl.ds(0, HEADS), pl.ds(0, 3)
    pl.semaphore_wait(barrier, len(peers))
    gone_d = [
        send(out_s.at[heads, 3, pixel_rows(at)], in_s.at[heads, 3, mine_rows], peer) for at, peer in clip
    ]
    loaded(5)
    packed = nn(hid1[...], w1[...]).astype(BF16)
    for n in range(3):
        for h in range(HEADS):
            out_s[h, n] = packed[:, (2 * n + h) * HD : (2 * n + h + 1) * HD]

    def send_head(h):
        return [
            send(out_s.at[h, first_kinds, pixel_rows(at)], in_s.at[h, first_kinds, mine_rows], peer)
            for at, peer in clip
        ]

    gone = [send_head(0)]

    order = (0, 4, 1, 5, 2, 6, 3, 7, 8, 12, 9, 13, 10, 14, 11, 15, 16, 17)
    own_tokens, sib_tokens = pl.ds(0, rows_of), pl.ds(rows_of, rows_of)

    def flip(src, dst, n):
        size = 4 * BLOCK_ROWS
        for top in range(0, features, size):
            turned = src[:, top : top + size].T
            for block in range(0, size, BLOCK_ROWS):
                for at, tile in enumerate(order):
                    dst[n, top + block + at * 16 : top + block + at * 16 + 16, 0:rows_of] = turned[
                        block + tile * 16 : block + tile * 16 + 16, :
                    ]
        return send(dst.at[n, :, own_tokens], dst.at[n, :, sib_tokens], sibling)

    shared1 = [flip(hid1, left1, 0), flip(g1, left1, 1)]
    departed(gone[0])
    gone.append(send_head(1))

    pixel_row = lax.bitwise_and(lax.broadcasted_iota(jnp.int32, (rows_of, rows_of), 0), pixels - 1)
    pixel_col = lax.bitwise_and(lax.broadcasted_iota(jnp.int32, (rows_of, rows_of), 1), pixels - 1)
    same_pixel = pixel_row == pixel_col
    came = []
    arrived(gone_d)
    for h in range(HEADS):
        in_s[h, :, mine_rows, :] = out_s[h, :, mine_rows, :]
        arrived(gone[h])
        query, key, value, d_out = [in_s[h, n] for n in range(UNITS)]
        p = softmax(query, key, same_pixel)
        out_p[h, 3] = nn(p.astype(BF16), value).astype(BF16)
        for n, part_of in enumerate(attend_back(query, key, value, p, d_out)):
            out_p[h, n] = part_of
        came.append([
            send(out_p.at[h, :, pixel_rows(at)], back.at[h, :, mine_rows], peer) for at, peer in clip
        ])
    shared0 = [flip(hid0, left0, 0)]
    for h in range(HEADS):
        back[h, :, mine_rows, :] = out_p[h, :, mine_rows, :]
        arrived(came[h])
    kinds = pl.ds(pl.multiple_of(2 * core, 2), 2)
    sib_kinds = pl.ds(pl.multiple_of(2 * (1 - core), 2), 2)
    shared1.append(send(back.at[heads, sib_kinds], sib_b1, sibling))

    def tile_for(z_at, hi_at, half_at):
        group = 2 * hi_at + half_at
        ahead = lax.max(36 * z_at + 35 - SLOT * group, 0)
        return lax.min(lax.div(ahead, 4 * SLOT), 4 - hi_at)

    z_half = lax.rem(z, 2)
    sources = [(hi_at, half_at) for hi_at in range(2) for half_at in range(2)]
    slot = lax.broadcasted_iota(jnp.int32, (2 * SLOT, 4 * SLOT), 0)
    tile_row = lax.broadcasted_iota(jnp.int32, (2 * SLOT, 4 * SLOT), 1)
    have = lax.bitwise_and(tile_row, SLOT - 1)
    for n, (hi_at, half_at) in enumerate(sources):
        top = 4 * SLOT * tile_for(z, hi_at, half_at) + SLOT * (2 * hi_at + half_at) - 36 * z
        have = jnp.where(lax.shift_right_logical(tile_row, 4) == n, have + top, have)
    within = lax.bitwise_and(slot, SLOT - 1)
    want = (2 * lax.shift_right_logical(slot, 4) + x_hi) * OWN + within
    pick = jnp.where((have == want) & (within < OWN), 1.0, 0.0).astype(BF16)

    def reduction(box, t, b):
        (_, xa, xc, xm, xb, xu, ya, yc, ym, yb, yu, x2, y2, tz, zr, zu, zx, zy, last_out, last_in,
         held, gather, merged, final) = box

        def rows(x_at, y_at, offset):
            start = (lax.rem(x_at, 2) * 4 + y_at) * BLOCK_ROWS + offset + X_ROWS * lax.div(x_at, 2)
            return pl.ds(pl.multiple_of(start, 16), X_ROWS)

        def x_src(a, b):
            return t.at[rows(a, b, 0)]

        def y_src(a, b):
            return t.at[rows(b, a, 2 * X_ROWS)]

        def total2(one, two):
            return (one.astype(F32) + two.astype(F32)).astype(BF16)

        def far_sends(me, src, into, right, left):
            far = turn(me, 2, 4)
            return (
                [send(src(far, b), into.at[b], right) for b in (0, 1)]
                + [send(src(far, b), into.at[b], left) for b in (2, 3)]
            )

        def near_sends(me, src, into, right, left):
            return (
                [send(src(turn(me, 1, 4), b), into.at[b], right) for b in (2, 3)]
                + [send(src(turn(me, 3, 4), b), into.at[b], left) for b in (0, 1)]
            )

        def relay(me, src, box_in, kept, into, far, right, left):
            outs = []
            for n in (0, 2, 1, 3):
                far[n].wait_recv()
                kept[n] = total2(box_in[n], src(turn(me, 1 if n < 2 else 3, 4), n)[...])
                outs.append(send(kept.at[n], into.at[n], right if n < 2 else left))
            return outs

        def finish(me, src, near, into, copies, result):
            arrived(copies)
            for b in range(4):
                result[b] = (
                    src(me, b)[...].astype(F32) + near[b].astype(F32) + into[b].astype(F32)
                ).astype(BF16)

        half = X_ROWS // 2

        def second_start(me, kept, into, ring):
            return [send(kept.at[turn(me, k, 4)], into.at[n], peer) for n, (k, peer) in enumerate(ring)]

        def second_finish(me, kept, into, copies, offset):
            arrived(copies)
            total = kept[me].astype(F32)
            for n in range(3):
                total = total + into[n].astype(F32)
            total = total.astype(BF16)
            for u in range(UNITS):
                for hf in range(2):
                    last_out[2 * u + hf, offset : offset + half, :] = total[
                        hf * half : (hf + 1) * half, u * HD : (u + 1) * HD
                    ]

        def start():
            x_far_sends = far_sends(x, x_src, xa, x_right, x_left)
            y_far_sends = far_sends(y, y_src, ya, y_right, y_left)
            for u in range(UNITS):
                for hf in range(2):
                    for a in range(8):
                        top = a * BLOCK_ROWS + 4 * X_ROWS + Z_ROWS * hf
                        tz[2 * u + hf, a] = t[top : top + Z_ROWS, u * HD : (u + 1) * HD]
            z_sends = [send(tz.at[turn(z, k, 8)], zr.at[k - 1], z_peers[k]) for k in z_order]
            yield
            x_near = near_sends(x, x_src, xb, x_right, x_left)
            y_near = near_sends(y, y_src, yb, y_right, y_left)
            yield
            x_relays = relay(x, x_src, xa, xm, xc, x_far_sends, x_right, x_left)
            y_relays = relay(y, y_src, ya, ym, yc, y_far_sends, y_right, y_left)
            yield
            finish(x, x_src, xb, xc, x_near + x_relays, xu)
            x_second = second_start(y, xu, x2, y_ring)
            finish(y, y_src, yb, yc, y_near + y_relays, yu)
            y_second = second_start(x, yu, y2, x_ring)
            arrived(z_sends)
            total = tz[z].astype(F32)
            for k in range(7):
                total = total + zr[k].astype(F32)
            zu[...] = total.astype(BF16)

            def quad(x_lo_at):
                return pl.ds(pl.multiple_of(x_lo_at * 4, 4), 4)

            z_first = [
                send(zu.at[quad(x_lo)], zx.at[0], x_far),
                send(zu.at[quad(1 - x_lo)], zx.at[1], x_right),
                send(zu.at[quad(1 - x_lo)], zx.at[2], x_left),
            ]
            yield
            second_finish(y, xu, x2, x_second, 0)
            second_finish(x, yu, y2, y_second, half)
            last = [send(last_out.at[turn(z, k, 8)], last_in.at[k - 1], z_peers[k]) for k in z_order]
            arrived(z_first)
            total = zu[quad(x_lo)].astype(F32)
            for n in range(3):
                total = total + zx[n].astype(F32)
            zx[3] = total.astype(BF16)
            z_second = [send(zx.at[3, turn(y, k, 4)], zy.at[n], peer) for n, (k, peer) in enumerate(y_ring)]
            yield
            arrived(last)
            total = last_out[z].astype(F32)
            for k in range(7):
                total = total + last_in[k].astype(F32)
            for k in range(4):
                held[k] = total[k * SLOT : (k + 1) * SLOT, :].astype(BF16)
            arrived(z_second)
            total = zx[3, y].astype(F32)
            for n in range(3):
                total = total + zy[n].astype(F32)
            held[4] = total.astype(BF16)
            tiles_out = {k: held.at[tile_for(turn(z, k, 8), x_hi, z_half)] for k in z_order}
            gathers = [send(tiles_out[k], gather.at[x_hi, z], z_peers[k]) for k in z_order]
            gathers += [send(tiles_out[k], gather.at[x_hi, z], far_z_peers[k]) for k in z_order]
            own_tile = held.at[tile_for(z, x_hi, z_half)]
            gathers.append(send(own_tile, gather.at[x_hi, z], x_far))
            gather[x_hi, z] = own_tile[...]
            yield
            arrived(gathers)
            tiles = jnp.concatenate(
                [
                    jnp.concatenate([gather[hi_at, 2 * u + half_at] for u in range(UNITS)], axis=1)
                    for hi_at, half_at in sources
                ],
                axis=0,
            )
            owned = nn(pick, tiles).astype(BF16)
            for n in range(2):
                merged[n] = owned[n * SLOT : (n + 1) * SLOT, :]
            swap = send(merged.at[1 - core], final, sibling)
            yield
            scale = 1.0 / math.sqrt(rows_of * lax.axis_size("seq") * lax.axis_size("rep"))
            same = merged[core].astype(F32) * scale
            arrived([swap])
            others = final[...].astype(F32) * scale
            cores = [jnp.where(core == 0, same, others), jnp.where(core == 0, others, same)]
            both = jnp.concatenate(cores, axis=1).astype(BF16)
            for i in range(OWN):
                qkv_ref[i, b : b + 1, :] = both[i : i + 1, : 6 * HD]
                att_ref[i, b : b + 1, :] = both[i : i + 1, 6 * HD :]
            yield

        return start()

    def weight_sums(t, left, own, theirs):
        for n in range(2):
            right = jnp.concatenate(
                [
                    jnp.concatenate([own[h, 2 * core + n] for h in range(HEADS)], axis=1),
                    jnp.concatenate([theirs[h, n] for h in range(HEADS)], axis=1),
                ],
                axis=0,
            )
            source = core if n == 1 else 0

            t[:, 2 * n * HD : 2 * (n + 1) * HD] = nn(left[source], right).astype(BF16)

    def input_back(src, weight):
        d_packed = jnp.concatenate([src[h, n] for n in range(3) for h in range(HEADS)], axis=1)

        def body(at):
            acc[:, at] = nt(d_packed, weight[at, :])

        by_columns(body)

    t1, t0 = boxes[1][0], boxes[0][0]
    arrived(shared1)
    weight_sums(t1, left1, back, sib_b1)
    steps1 = reduction(boxes[1], t1, 1)
    next(steps1)
    input_back(back, w1)

    d_mid_ref = hid1

    def temporal_back(at):
        normed, inv_std = normalize(mid[at, :].astype(F32))
        term = norm_back(acc[at, :] * (1.0 + mod(scale1)), normed, inv_std)
        d_mid = (cot_ref[at, :].astype(F32) + term).astype(BF16)
        d_mid_ref[at, :] = d_mid
        g0[at, :] = (mod(gate0) * d_mid.astype(F32)).astype(BF16)

    by_rows(temporal_back)
    next(steps1)

    shared0.append(flip(g0, left0, 1))
    d_att0 = nt(g0[...], wo0[...]).astype(BF16)
    for h in range(HEADS):
        grads = attend_back(part(0, h), part(1, h), part(2, h), probs[h], d_att0[:, h * HD : (h + 1) * HD])
        for n, part_of in enumerate(grads):
            b0[h, n] = part_of
    shared0.append(send(b0.at[heads, sib_kinds], sib_b0, sibling))
    next(steps1)
    arrived(shared0)
    weight_sums(t0, left0, b0, sib_b0)
    steps0 = reduction(boxes[0], t0, 0)
    next(steps0)

    def spatial_back(at):
        normed, inv_std = normalize(x_ref[at, :].astype(F32))
        term = norm_back(acc[at, :] * (1.0 + mod(scale0)), normed, inv_std)
        grad_ref[at, :] = (d_mid_ref[at, :].astype(F32) + term).astype(BF16)

    input_back(b0, w0)
    next(steps0)
    by_rows(spatial_back)
    next(steps0)
    next(steps1)
    next(steps0)
    next(steps1)
    next(steps0)
    next(steps1)
    next(steps0)
    next(steps1)
    next(steps0)
    next(steps1)
    next(steps0)
    for copy in used:
        if not any(copy is other for other in gone_already):
            copy.wait_send()


def whole(tokens, ids, cotangent, modulation, w_qkv, w_out):
    _, rows, features = tokens.shape
    inner = HEADS * HD

    def vmem(*shape, dtype=BF16):
        return pltpu.VMEM(shape, dtype)

    full = lambda: vmem(rows, features)
    pooled = lambda: vmem(2, features, 2 * rows)
    units = lambda: vmem(HEADS, UNITS, rows, HD)
    ring = [vmem(4, X_ROWS, WIDE) for _ in range(5)]
    second = [vmem(3, X_ROWS, WIDE)]
    reduction = (
        [vmem(features, WIDE)] + ring + ring + second + second + [
            vmem(8, 8, Z_ROWS, HD), vmem(7, 8, Z_ROWS, HD), vmem(8, Z_ROWS, HD),
            vmem(4, 4, Z_ROWS, HD), vmem(3, Z_ROWS, HD),
            vmem(8, X_ROWS, HD), vmem(7, X_ROWS, HD),
            vmem(5, SLOT, HD), vmem(2, 8, SLOT, HD), vmem(2, SLOT, WIDE), vmem(SLOT, WIDE),
        ]
    )
    scratch = [
        full(), full(), vmem(features, 3 * inner), vmem(features, 3 * inner),
        vmem(inner, features), vmem(inner, features),
        full(), full(), full(), full(), full(), vmem(rows, features, dtype=F32),
        vmem(rows, 3 * inner), vmem(HEADS, rows, rows, dtype=F32), vmem(rows, inner),
    ] + [vmem(1, rows, dtype=jnp.int32), vmem(6, features, dtype=F32), pooled(), pooled()] + [units() for _ in range(5)] + [
        vmem(HEADS, 2, rows, HD), vmem(HEADS, 2, rows, HD),
    ] + reduction + reduction + [
        pltpu.SemaphoreType.DMA((20,)),
        pltpu.SemaphoreType.DMA((176,)),
        pltpu.SemaphoreType.DMA((176,)),
    ]
    in_vmem = pl.BlockSpec(memory_space=pltpu.VMEM)
    anywhere = pl.BlockSpec(memory_space=pl.ANY)
    return pl.pallas_call(
        whole_kernel,
        out_shape=(
            pltpu.VMEM((rows, features), BF16),
            pltpu.VMEM((OWN, 2, 3 * inner), BF16),
            pltpu.VMEM((OWN, 2, inner), BF16),
        ),
        in_specs=[anywhere] * 6,
        out_specs=(in_vmem, in_vmem, in_vmem),
        scratch_shapes=scratch,
        compiler_params=pltpu.CompilerParams(
            collective_id=0, has_side_effects=True, vmem_limit_bytes=60 * 2**20
        ),
    )(tokens, ids, cotangent, modulation, w_qkv, w_out)


def local(tokens, window_ids, cotangent, modulation, w_qkv, w_out):
    d_tokens, qkv, out = whole(tokens, window_ids, cotangent, modulation, w_qkv, w_out)
    return (d_tokens[None], qkv.transpose(1, 0, 2), out.transpose(1, 2, 0))


def solution(mesh):
    in_specs = (P("rep", "seq", None), P("rep", "seq"), P("rep", "seq", None), P(), P(), P())
    out_specs = (
        P("rep", "seq", None),
        P(None, ("seq", "rep"), None),
        P(None, None, ("seq", "rep")),
    )
    return jax.shard_map(local, mesh=mesh, in_specs=in_specs, out_specs=out_specs, check_vma=False)
```
